128 devices in a mesh: ctx: 8 (over y_lo, x), fsdp: 16 (over z, y_hi, core).
Axes of the slice: x: 4, y: 4 (y_hi: 2, y_lo: 2; y = y_hi * 2 + y_lo), z: 4, core: 2. Of those that a mesh axis runs over, the one named last changes fastest.
Arguments:
- tokens: bfloat16 [16, 2048, 896], P('fsdp', 'ctx'), may hold values from -6 to 6
- cotangent: bfloat16 [16, 2048, 896], P('fsdp', 'ctx'), may hold values from -6 to 6
- layout: int32 [16, 32], P('fsdp'), may hold values from 0 to 31, as said below
- w_query: float32 [896, 896], P(('ctx', 'fsdp')), may hold values from -0.1875 to 0.1875
- m_query: float32 [896, 896], P(('ctx', 'fsdp')), may hold values from -1 to 1
- v_query: float32 [896, 896], P(('ctx', 'fsdp')), may hold values from 0 to 1
- w_key: float32 [896, 128], P(('ctx', 'fsdp')), may hold values from -0.1875 to 0.1875
- m_key: float32 [896, 128], P(('ctx', 'fsdp')), may hold values from -1 to 1
- v_key: float32 [896, 128], P(('ctx', 'fsdp')), may hold values from 0 to 1
- w_value: float32 [896, 128], P(('ctx', 'fsdp')), may hold values from -0.1875 to 0.1875
- m_value: float32 [896, 128], P(('ctx', 'fsdp')), may hold values from -1 to 1
- v_value: float32 [896, 128], P(('ctx', 'fsdp')), may hold values from 0 to 1
- w_out: float32 [896, 896], P(('ctx', 'fsdp')), may hold values from -1 to 1
- m_out: float32 [896, 896], P(('ctx', 'fsdp')), may hold values from -1 to 1
- v_out: float32 [896, 896], P(('ctx', 'fsdp')), may hold values from 0 to 1
- w_gate: float32 [896, 4864], P(('ctx', 'fsdp')), may hold values from -0.1875 to 0.1875
- m_gate: float32 [896, 4864], P(('ctx', 'fsdp')), may hold values from -1 to 1
- v_gate: float32 [896, 4864], P(('ctx', 'fsdp')), may hold values from 0 to 1
- w_up: float32 [896, 4864], P(('ctx', 'fsdp')), may hold values from -0.1875 to 0.1875
- m_up: float32 [896, 4864], P(('ctx', 'fsdp')), may hold values from -1 to 1
- v_up: float32 [896, 4864], P(('ctx', 'fsdp')), may hold values from 0 to 1
- w_down: float32 [896, 4864], P(('ctx', 'fsdp')), may hold values from -0.078125 to 0.078125
- m_down: float32 [896, 4864], P(('ctx', 'fsdp')), may hold values from -1 to 1
- v_down: float32 [896, 4864], P(('ctx', 'fsdp')), may hold values from 0 to 1
- w_vectors: float32 [2944], P(('ctx', 'fsdp')), may hold values from -1 to 4
- m_vectors: float32 [2944], P(('ctx', 'fsdp')), may hold values from -1 to 1
- v_vectors: float32 [2944], P(('ctx', 'fsdp')), may hold values from 0 to 1
Outputs:
- output: bfloat16 [16, 2048, 896], P('fsdp', 'ctx')
- input_grad: float32 [16, 2048, 896], P('fsdp', 'ctx')
- grad_norm: float32 [], replicated
- w_query_new: float32 [896, 896], P(('ctx', 'fsdp'))
- m_query_new: float32 [896, 896], P(('ctx', 'fsdp'))
- v_query_new: float32 [896, 896], P(('ctx', 'fsdp'))
- w_query_copy: bfloat16 [896, 896], P(('ctx', 'fsdp'))
- w_key_new: float32 [896, 128], P(('ctx', 'fsdp'))
- m_key_new: float32 [896, 128], P(('ctx', 'fsdp'))
- v_key_new: float32 [896, 128], P(('ctx', 'fsdp'))
- w_key_copy: bfloat16 [896, 128], P(('ctx', 'fsdp'))
- w_value_new: float32 [896, 128], P(('ctx', 'fsdp'))
- m_value_new: float32 [896, 128], P(('ctx', 'fsdp'))
- v_value_new: float32 [896, 128], P(('ctx', 'fsdp'))
- w_value_copy: bfloat16 [896, 128], P(('ctx', 'fsdp'))
- w_out_new: float32 [896, 896], P(('ctx', 'fsdp'))
- m_out_new: float32 [896, 896], P(('ctx', 'fsdp'))
- v_out_new: float32 [896, 896], P(('ctx', 'fsdp'))
- w_out_copy: bfloat16 [896, 896], P(('ctx', 'fsdp'))
- w_gate_new: float32 [896, 4864], P(('ctx', 'fsdp'))
- m_gate_new: float32 [896, 4864], P(('ctx', 'fsdp'))
- v_gate_new: float32 [896, 4864], P(('ctx', 'fsdp'))
- w_gate_copy: bfloat16 [896, 4864], P(('ctx', 'fsdp'))
- w_up_new: float32 [896, 4864], P(('ctx', 'fsdp'))
- m_up_new: float32 [896, 4864], P(('ctx', 'fsdp'))
- v_up_new: float32 [896, 4864], P(('ctx', 'fsdp'))
- w_up_copy: bfloat16 [896, 4864], P(('ctx', 'fsdp'))
- w_down_new: float32 [896, 4864], P(('ctx', 'fsdp'))
- m_down_new: float32 [896, 4864], P(('ctx', 'fsdp'))
- v_down_new: float32 [896, 4864], P(('ctx', 'fsdp'))
- w_down_copy: bfloat16 [896, 4864], P(('ctx', 'fsdp'))
- w_vectors_new: float32 [2944], P(('ctx', 'fsdp'))
- m_vectors_new: float32 [2944], P(('ctx', 'fsdp'))
- v_vectors_new: float32 [2944], P(('ctx', 'fsdp'))
- w_vectors_copy: bfloat16 [2944], P(('ctx', 'fsdp'))
The draws below stay inside these ranges and needn't reach their ends.
Inputs may be any that keep to these rules, and one draw needn't show every extreme that they name: `layout`: each row orders all 32 pieces of its group, each once.
All inputs are finite; a program needn't handle non-finite values.
Results may differ from the reference program's by a relative error of at most 0.03.
Values may be sent and summed in bfloat16 or wider, within the bound.
A program may use at most 192 MiB of HBM per device.

```python
import math
import jax
import jax.numpy as jnp
from jax import lax

D = 896
HEADS = 14
KV_HEADS = 2
HD = 64
FF = 4864
PROMPT = 1024
CONT = 512
PIECE = 64
KBLK = 512
STEP = 10
GROUP_TOK = 2048
GROUPS = 16
NP = 32
VEC = 2944
PARAMS = 14912384
N_CTX = 8
N_FSDP = 16


def moment_one(key, array_shape, boost_by):
    typical = boost_by / math.sqrt(PARAMS)
    return jax.random.uniform(key, array_shape, jnp.float32, -1.0, 1.0) * (0.19 * typical)


def moment_two(key, array_shape, boost_by):
    typical = boost_by / math.sqrt(PARAMS)
    spread = jnp.exp(jax.random.uniform(key, array_shape, jnp.float32, 0.0, math.log(4.0)))
    return spread * (0.0526 * typical * typical)


def draw_layout(key, part):
    key = jax.random.fold_in(key, 5)
    prompt_pieces = PROMPT // PIECE

    def one_row(row_key):
        ordering = jax.random.permutation(row_key, NP).astype(jnp.int32)
        where_first = jnp.argmax(ordering == 0).astype(jnp.int32)
        ordering = ordering.at[where_first].set(ordering[0]).at[0].set(0)
        where_last = jnp.argmax(ordering == prompt_pieces - 1).astype(jnp.int32)
        ordering = ordering.at[where_last].set(ordering[NP - 1]).at[NP - 1].set(prompt_pieces - 1)
        return ordering
    return jax.vmap(one_row)(jax.random.split(key, GROUPS))


def draw_w_vectors(key, part):
    key = jax.random.fold_in(key, 7)
    rise_by = 3.0
    devices = N_CTX * N_FSDP
    device_of = jnp.arange(D, dtype=jnp.int32) // (D // devices)
    outer_pos = (device_of // N_FSDP).astype(jnp.float32) / max(N_CTX - 1, 1)
    inner_pos = (device_of % N_FSDP).astype(jnp.float32) / max(N_FSDP - 1, 1)
    gain_scale = 0.6 * jnp.exp(0.5 * math.log(rise_by) * (outer_pos + inner_pos))
    sub_keys = jax.random.split(key, 2)
    gain_rows = gain_scale[None, :] * jax.random.uniform(sub_keys[0], (2, D), jnp.float32, 0.8, 1.25)
    biases = jax.random.uniform(sub_keys[1], (HEADS * HD + 2 * KV_HEADS * HD,), jnp.float32, -0.6, 0.6)
    return jnp.concatenate([gain_rows.reshape(2 * D), biases])


def draw_m_query(key, part):
    key = jax.random.fold_in(key, 21)
    return moment_one(key, (D, HEADS * HD), 1.0)


def draw_v_query(key, part):
    key = jax.random.fold_in(key, 22)
    return moment_two(key, (D, HEADS * HD), 1.0)


def draw_m_key(key, part):
    key = jax.random.fold_in(key, 23)
    return moment_one(key, (D, KV_HEADS * HD), 1.0)


def draw_v_key(key, part):
    key = jax.random.fold_in(key, 24)
    return moment_two(key, (D, KV_HEADS * HD), 1.0)


def draw_m_value(key, part):
    key = jax.random.fold_in(key, 25)
    return moment_one(key, (D, KV_HEADS * HD), 1.0)


def draw_v_value(key, part):
    key = jax.random.fold_in(key, 26)
    return moment_two(key, (D, KV_HEADS * HD), 1.0)


def draw_m_out(key, part):
    key = jax.random.fold_in(key, 27)
    return moment_one(key, (HEADS * HD, D), 1.0)


def draw_v_out(key, part):
    key = jax.random.fold_in(key, 28)
    return moment_two(key, (HEADS * HD, D), 1.0)


def draw_m_gate(key, part):
    key = jax.random.fold_in(key, 29)
    return moment_one(key, (D, FF), 1.0)


def draw_v_gate(key, part):
    key = jax.random.fold_in(key, 30)
    return moment_two(key, (D, FF), 1.0)


def draw_m_up(key, part):
    key = jax.random.fold_in(key, 31)
    return moment_one(key, (D, FF), 1.0)


def draw_v_up(key, part):
    key = jax.random.fold_in(key, 32)
    return moment_two(key, (D, FF), 1.0)


def draw_m_down(key, part):
    key = jax.random.fold_in(key, 33)
    return moment_one(key, (D, FF), 1.0)


def draw_v_down(key, part):
    key = jax.random.fold_in(key, 34)
    return moment_two(key, (D, FF), 1.0)


def draw_m_vectors(key, part):
    key = jax.random.fold_in(key, 35)
    return moment_one(key, (VEC,), 3.0)


def draw_v_vectors(key, part):
    key = jax.random.fold_in(key, 36)
    return moment_two(key, (VEC,), 3.0)


def block_scale(stream_key, shape, cuts, low, largest):
    def one(dim, parts):
        heights = jax.random.uniform(jax.random.fold_in(jax.random.fold_in(stream_key, 6), dim), (parts,), jnp.float32, low / len(cuts), largest / len(cuts))
        return jnp.repeat(jnp.exp(heights), shape[dim] // parts).reshape((-1,) + (1,) * (len(shape) - dim - 1))

    factor_of = one(*cuts[0])
    for cut in cuts[1:]:
        factor_of = factor_of * one(*cut)
    return factor_of


def centred(rng, extent, scale, reach, shards=(), kind=jnp.bfloat16):
    factor_of = block_scale(rng, extent, shards, -0.22, 0.18) if shards else 1.0
    values = jax.random.normal(rng, extent, jnp.float32) * scale * factor_of
    return jnp.minimum(jnp.maximum(values, -reach), reach).astype(kind)


def setup_inputs(seed: int = 0) -> dict:
    key_of = jax.random.split(jax.random.key(seed), 28)
    tokens = centred(key_of[0], (GROUPS, GROUP_TOK, D), 1.0, 6.0, ((0, 16), (1, 8)))
    cotangent = centred(key_of[1], (GROUPS, GROUP_TOK, D), 1.0, 6.0, ((0, 16), (1, 8)))
    layout = draw_layout(jax.random.fold_in(key_of[27], 71), 0)
    w_query = centred(key_of[3], (D, HEADS * HD), D ** -0.5, 0.1875, ((0, 128),), jnp.float32)
    m_query = draw_m_query(jax.random.fold_in(key_of[27], 71), 0)
    v_query = draw_v_query(jax.random.fold_in(key_of[27], 71), 0)
    w_key = centred(key_of[6], (D, KV_HEADS * HD), D ** -0.5, 0.1875, ((0, 128),), jnp.float32)
    m_key = draw_m_key(jax.random.fold_in(key_of[27], 71), 0)
    v_key = draw_v_key(jax.random.fold_in(key_of[27], 71), 0)
    w_value = centred(key_of[9], (D, KV_HEADS * HD), D ** -0.5, 0.1875, ((0, 128),), jnp.float32)
    m_value = draw_m_value(jax.random.fold_in(key_of[27], 71), 0)
    v_value = draw_v_value(jax.random.fold_in(key_of[27], 71), 0)
    w_out = centred(key_of[12], (HEADS * HD, D), (max(HEADS * HD * 64 // GROUP_TOK, 8)) ** -0.5, 1.0, ((0, 128),), jnp.float32)
    m_out = draw_m_out(jax.random.fold_in(key_of[27], 71), 0)
    v_out = draw_v_out(jax.random.fold_in(key_of[27], 71), 0)
    w_gate = centred(key_of[15], (D, FF), D ** -0.5, 0.1875, ((0, 128),), jnp.float32)
    m_gate = draw_m_gate(jax.random.fold_in(key_of[27], 71), 0)
    v_gate = draw_v_gate(jax.random.fold_in(key_of[27], 71), 0)
    w_up = centred(key_of[18], (D, FF), D ** -0.5, 0.1875, ((0, 128),), jnp.float32)
    m_up = draw_m_up(jax.random.fold_in(key_of[27], 71), 0)
    v_up = draw_v_up(jax.random.fold_in(key_of[27], 71), 0)
    w_down = centred(key_of[21], (D, FF), FF ** -0.5, 0.078125, ((0, 128),), jnp.float32)
    m_down = draw_m_down(jax.random.fold_in(key_of[27], 71), 0)
    v_down = draw_v_down(jax.random.fold_in(key_of[27], 71), 0)
    w_vectors = draw_w_vectors(jax.random.fold_in(key_of[27], 71), 0)
    m_vectors = draw_m_vectors(jax.random.fold_in(key_of[27], 71), 0)
    v_vectors = draw_v_vectors(jax.random.fold_in(key_of[27], 71), 0)
    return {"tokens": tokens, "cotangent": cotangent, "layout": layout, "w_query": w_query, "m_query": m_query, "v_query": v_query, "w_key": w_key, "m_key": m_key, "v_key": v_key, "w_value": w_value, "m_value": m_value, "v_value": v_value, "w_out": w_out, "m_out": m_out, "v_out": v_out, "w_gate": w_gate, "m_gate": m_gate, "v_gate": v_gate, "w_up": w_up, "m_up": m_up, "v_up": v_up, "w_down": w_down, "m_down": m_down, "v_down": v_down, "w_vectors": w_vectors, "m_vectors": m_vectors, "v_vectors": v_vectors}


EPS_NORM = 1e-06
THETA = 1000000.0
CLIP = 1.0
BETA_ONE = 0.9
BETA_TWO = 0.95
ADAM_EPS = 1e-08
STEP_RATES = (0.02, 0.02, 0.02, 0.2, 0.02, 0.02, 0.02, 0.5)
DECAY = 0.1
MASKED = -1e+30
HIGH = lax.Precision.HIGHEST

@jax.custom_vjp
def low(v):
    return lax.optimization_barrier(v.astype(jnp.bfloat16)).astype(jnp.float32)

@jax.custom_vjp
def low_back(v):
    return v

def low_keep(v):
    return (low(v), None)

def low_pass(kept, grad):
    return (grad,)

def back_keep(v):
    return (v, None)

def back_low(kept, grad):
    return (low(grad),)
low.defvjp(low_keep, low_pass)
low_back.defvjp(back_keep, back_low)

def low_plain(values):
    return lax.optimization_barrier(values.astype(jnp.bfloat16)).astype(jnp.float32)

def token_tables(layout):
    slot_piece = jnp.repeat(layout, PIECE, axis=1)
    offsets = jnp.tile(jnp.arange(PIECE, dtype=jnp.int32), layout.shape[1])
    prompt_pieces = PROMPT // PIECE
    per_cont = CONT // PIECE
    later = slot_piece - prompt_pieces
    in_prompt = slot_piece < prompt_pieces
    seq_ids = jnp.where(in_prompt, 0, later // per_cont + 1).astype(jnp.int32)
    places = jnp.where(in_prompt, slot_piece * PIECE, PROMPT + later % per_cont * PIECE) + offsets[None, :]
    return (seq_ids, places.astype(jnp.int32))

def rms_norm(row_data, gain_vec):
    return row_data * lax.rsqrt(lax.optimization_barrier(jnp.mean(row_data * row_data, axis=-1, keepdims=True)) + EPS_NORM) * gain_vec

def rotate(values, places):
    half_dim = HD // 2
    frequency = THETA ** (-(jnp.arange(half_dim, dtype=jnp.float32) * (2.0 / HD)))
    angles = places.astype(jnp.float32)[..., None] * frequency
    cosine = jnp.cos(angles)[..., None, :]
    sine_part = jnp.sin(angles)[..., None, :]
    front_half = values[..., :half_dim]
    back_half = values[..., half_dim:]
    return jnp.concatenate([front_half * cosine - back_half * sine_part, back_half * cosine + front_half * sine_part], axis=-1)

def product(left, right):
    return jnp.dot(left, right, precision=HIGH, preferred_element_type=jnp.float32)

def attend_group(group_items):
    query_grp, key_grp, value_grp, seq_grp, pos_grp = group_items
    repeat = HEADS // KV_HEADS
    block_count = GROUP_TOK // KBLK
    query_blocks = query_grp.reshape(block_count, KBLK, KV_HEADS, repeat, HD)
    seq_blocks = seq_grp.reshape(block_count, KBLK)
    pos_blocks = pos_grp.reshape(block_count, KBLK)

    def one_block(block_items):
        query_blk, seq_query, pos_query = block_items
        scores = jnp.einsum('qgrd,kgd->grqk', query_blk, key_grp, precision=HIGH) * HD ** (-0.5)
        scores = low_back(scores)
        allowed = (pos_grp[None, :] <= pos_query[:, None]) & ((seq_grp[None, :] == 0) | (seq_grp[None, :] == seq_query[:, None]))
        scores = jnp.where(allowed[None, None], scores, MASKED)
        probabilities = jax.nn.softmax(scores, axis=-1)
        return jnp.einsum('grqk,kgd->qgrd', low(probabilities), value_grp, precision=HIGH)
    outputs = lax.map(jax.checkpoint(one_block), (query_blocks, seq_blocks, pos_blocks))
    return outputs.reshape(GROUP_TOK, HEADS * HD)

def adam_step(master, first_moment, second_moment, gradient, factor, step_rate, weight_decay):
    clipped = gradient * factor
    first_new = BETA_ONE * first_moment + (1.0 - BETA_ONE) * clipped
    second_new = BETA_TWO * second_moment + (1.0 - BETA_TWO) * clipped * clipped
    direction = first_new / (1.0 - BETA_ONE ** STEP) / (jnp.sqrt(second_new / (1.0 - BETA_TWO ** STEP)) + ADAM_EPS)
    master_new = master - step_rate * (direction + weight_decay * master)
    return (master_new, first_new, second_new, master_new.astype(jnp.bfloat16))

def reference(tokens, cotangent, layout, w_query, m_query, v_query, w_key, m_key, v_key, w_value, m_value, v_value, w_out, m_out, v_out, w_gate, m_gate, v_gate, w_up, m_up, v_up, w_down, m_down, v_down, w_vectors, m_vectors, v_vectors):
    seq_ids, places = token_tables(layout)
    masters = (w_query, w_key, w_value, w_out, w_gate, w_up, w_down, w_vectors)
    working = [low_plain(master) for master in masters]
    repeat = HEADS // KV_HEADS
    query_width = HEADS * HD
    kv_width = KV_HEADS * HD

    def forward(inputs, query_w, key_w, value_w, out_w, gate_w, up_w, down_w, vector_w):
        gain_attn = vector_w[:D]
        gain_mlp = vector_w[D:2 * D]
        bias_query = vector_w[2 * D:2 * D + query_width]
        bias_key = vector_w[2 * D + query_width:2 * D + query_width + kv_width]
        bias_value = vector_w[2 * D + query_width + kv_width:]
        row_data = inputs.reshape(GROUPS * GROUP_TOK, D)
        normed_one = low(rms_norm(row_data, gain_attn))
        query_pre = low_back(product(normed_one, query_w) + bias_query)
        key_pre = low_back(product(normed_one, key_w) + bias_key)
        value_pre = low_back(product(normed_one, value_w) + bias_value)
        queries = low(rotate(query_pre.reshape(GROUPS, GROUP_TOK, HEADS, HD), places))
        queries = queries.reshape(GROUPS, GROUP_TOK, KV_HEADS, repeat, HD)
        keys_all = low(rotate(key_pre.reshape(GROUPS, GROUP_TOK, KV_HEADS, HD), places))
        values_all = low(value_pre.reshape(GROUPS, GROUP_TOK, KV_HEADS, HD))
        attended = lax.map(attend_group, (queries, keys_all, values_all, seq_ids, places))
        attended = low(low_back(attended.reshape(GROUPS * GROUP_TOK, query_width)))
        mixed = row_data + low_back(product(attended, out_w))
        normed_two = low(rms_norm(mixed, gain_mlp))
        gate_pre = low_back(product(normed_two, gate_w))
        up_pre = low_back(product(normed_two, up_w))
        hidden = low(jax.nn.silu(gate_pre) * up_pre)
        result = mixed + low_back(product(hidden, down_w.T))
        return result.reshape(GROUPS, GROUP_TOK, D)
    output, pullback = jax.vjp(forward, tokens.astype(jnp.float32), *working)
    gradients = pullback(cotangent.astype(jnp.float32))
    input_grad = gradients[0]
    weight_grads = gradients[1:]
    square_sum = jnp.zeros((), jnp.float32)
    for gradient in weight_grads:
        square_sum = square_sum + jnp.sum(gradient * gradient)
    grad_norm = jnp.sqrt(square_sum)
    factor = CLIP / jnp.maximum(grad_norm, CLIP)
    firsts = (m_query, m_key, m_value, m_out, m_gate, m_up, m_down, m_vectors)
    seconds = (v_query, v_key, v_value, v_out, v_gate, v_up, v_down, v_vectors)
    results = [output.astype(jnp.bfloat16), input_grad, grad_norm]
    for number in range(8):
        step_rate = STEP_RATES[number]
        weight_decay = 0.0 if number == 7 else DECAY
        results.extend(adam_step(masters[number], firsts[number], seconds[number], weight_grads[number], factor, step_rate, weight_decay))
    return tuple(results)
```

```python
import jax
import jax.numpy as jnp
import numpy as np
from jax import lax
from jax.experimental import pallas as pl
from jax.experimental.pallas import tpu as pltpu
from jax.sharding import PartitionSpec as P

HEADS = 14
KV_HEADS = 2
HD = 64
PROMPT = 1024
CONT = 512
PIECE = 64
KBLK = 512
STEP = 10
D = 896
FF = 4864
TOK = 256
DP = 1024
FB = 640
QKV = 1152
ATT = 1152
FFN = 3 * FB
COLS = ATT + FFN
NVEC = 23
LANES = 2 * DP + QKV
LOG_E = 1.4426950408889634
A1 = 640
A2 = 512
HALF = COLS // 2

EPS_NORM = 1e-06
THETA = 1000000.0
CLIP = 1.0
BETA_ONE = 0.9
BETA_TWO = 0.95
ADAM_EPS = 1e-08
STEP_RATES = (0.02, 0.02, 0.02, 0.2, 0.02, 0.02, 0.02, 0.5)
DECAY = 0.1
MASKED = -1e30
MESH = pl.DeviceIdType.MESH
BF = jnp.bfloat16
F32 = jnp.float32
VMEM_LIMIT = 60 * 1024 * 1024


def owner_order():
    order = np.zeros((DP,), np.int32) - 1
    for x in range(4):
        for y in range(4):
            for z in range(4):
                for core in range(2):
                    p = z * 2 + core
                    owner = ((y % 2) * 4 + x) * 16 + z * 4 + (y // 2) * 2 + core
                    block = y * 4 + x if p < 4 else x * 4 + y
                    start = (p // 4) * 512 + block * 32 + (p % 4) * 8
                    order[start : start + 7] = np.arange(7 * owner, 7 * owner + 7)
    return order


def spread_matrix():
    order = owner_order()
    out = np.zeros((D, DP), np.float32)
    for column in range(DP):
        if order[column] >= 0:
            out[order[column], column] = 1.0
    return out

def vector_tables():
    order = owner_order()
    natural = np.concatenate([order, np.where(order < 0, -1, order + D), np.arange(2 * D, 2 * D + QKV)])
    owner_at = np.zeros((128,), np.int32)
    pick = np.zeros((128, DP), np.float32)
    for n in range(128):
        c, f = n // 16, n % 16
        owner_at[n] = ((f // 2 % 2 * 2 + c // 4) * 4 + c % 4) * 8 + f // 4 * 2 + f % 2
        pick[owner_at[n], np.nonzero(order == 7 * n)[0][0] + 7] = 1.0
    holds = np.zeros((128, LANES), np.float32)
    spots = np.zeros((128, LANES), np.float32)
    for lane in range(LANES):
        if natural[lane] >= 0:
            holds[owner_at[natural[lane] // NVEC], lane] = 1.0
            spots[natural[lane] % NVEC, lane] = 1.0
    return pick, spots, holds


def turn_tables():
    frequency = THETA ** (-(np.arange(HD // 2) * (2.0 / HD)))
    out = np.zeros((4, 64, 128), np.float32)
    for n, step in enumerate((PIECE, 1)):
        angles = np.arange(64)[:, None] * float(step) * frequency[None, :]
        out[2 * n] = np.tile(np.cos(angles), (1, 4))
        out[2 * n + 1] = np.tile(np.sin(angles), (1, 4))
    return out


def place():
    c = lax.axis_index("ctx")
    f = lax.axis_index("fsdp")
    return c % 4, (f // 2) % 2 * 2 + c // 4, f // 4, f % 2


def device(x, y, z, core):
    return {"ctx": y % 2 * 4 + x, "fsdp": z * 4 + y // 2 * 2 + core}


def x_peer(me, k):
    x, y, z, core = me
    return device((x + k) % 4, y, z, core)


def y_peer(me, k):
    x, y, z, core = me
    return device(x, (y + k) % 4, z, core)


def z_peer(me, k):
    x, y, z, core = me
    return device(x, y, (z + k) % 4, core)


def pair_peer(me):
    x, y, z, core = me
    return device(x, y // 2 * 2 + 1 - y % 2, z, core)


def other_core(me):
    x, y, z, core = me
    return device(x, y, z, 1 - core)


def line_peer(me, k):
    x, y, z, core = me
    t = (z * 2 + core + k) % 8
    return t, device(x, y, t // 2, t % 2)


def copy(src, dst, send, recv, target):
    return pltpu.make_async_remote_copy(
        src_ref=src, dst_ref=dst, send_sem=send, recv_sem=recv, device_id=target, device_id_type=MESH
    )


def greet(targets):
    barrier = pltpu.get_barrier_semaphore()
    for target in targets:
        pl.semaphore_signal(barrier, inc=1, device_id=target, device_id_type=MESH)
    pl.semaphore_wait(barrier, len(targets))


def line_targets(me):
    return [line_peer(me, k)[1] for k in range(1, 8)]


def ring_targets(me, peer):
    return [peer(me, 1), peer(me, 3)]


class Ring:
    def __init__(self, me, axis, block, half, send, recv):
        self.at = me[axis]
        self.up = (x_peer, y_peer, z_peer)[axis](me, 1)
        self.down = (x_peer, y_peer, z_peer)[axis](me, 3)
        self.half, self.send, self.recv = half, send, recv
        self.close = False

    def one(self, number, arriving=False):
        a = self.at
        ahead, behind, far = (a + 1) % 4, (a + 3) % 4, (a + 2) % 4
        half = (0, 1, 1, 0, 0, 1)[number]
        if arriving:
            t = (behind, behind, ahead, ahead, far, far)[number]
        else:
            t = (a, a, a, a, behind, ahead)[number]
        target = (self.up, self.up, self.down, self.down, self.up, self.down)[number]
        ref = self.half(t, half)
        return copy(ref, ref, self.send.at[number], self.recv.at[number], target)

    def start(self):
        for number in (0, 2, 1, 3):
            self.one(number).start()

    def relay(self):
        self.one(0, True).wait_recv()
        self.one(4).start()
        self.one(2, True).wait_recv()
        self.one(5).start()

    def near(self):
        self.close = True
        self.one(1, True).wait_recv()
        self.one(3, True).wait_recv()

    def finish(self):
        if not self.close:
            self.near()
        self.one(4, True).wait_recv()
        self.one(5, True).wait_recv()

    def drain(self):
        for number in range(6):
            self.one(number).wait_send()


def add_into(ref, other):
    ref[...] = ref[...] + other[...]


class RingSum:
    def __init__(self, me, axis, block, half, tmp, land, land_half, send, recv):
        self.at = me[axis]
        self.up = (x_peer, y_peer, z_peer)[axis](me, 1)
        self.down = (x_peer, y_peer, z_peer)[axis](me, 3)
        self.block, self.half, self.tmp = block, half, tmp
        self.land, self.land_half = land, land_half
        self.send, self.recv = send, recv

    def one(self, number):
        far, ahead, behind = (self.at + 2) % 4, (self.at + 1) % 4, (self.at + 3) % 4
        src, dst, target = (
            (self.half(far, 0), self.tmp(0), self.up), (self.half(far, 1), self.tmp(1), self.down),
            (self.half(ahead, 1), self.land_half(0, 1), self.up),
            (self.half(behind, 0), self.land_half(1, 0), self.down),
            (self.half(ahead, 0), self.land_half(0, 0), self.up),
            (self.half(behind, 1), self.land_half(1, 1), self.down),
        )[number]
        return copy(src, dst, self.send.at[number], self.recv.at[number], target)

    def start_far(self):
        self.one(0).start()
        self.one(1).start()

    def start_near(self):
        self.one(2).start()
        self.one(3).start()

    def start(self):
        self.start_far()
        self.start_near()

    def relay(self):
        ahead, behind = (self.at + 1) % 4, (self.at + 3) % 4
        self.one(0).wait_recv()
        add_into(self.half(ahead, 0), self.tmp(0))
        self.one(4).start()
        self.one(1).wait_recv()
        add_into(self.half(behind, 1), self.tmp(1))
        self.one(5).start()

    def finish(self):
        for number in range(2, 6):
            self.one(number).wait_recv()
        own = self.block(self.at)[...].astype(F32)
        return own + self.land(0)[...].astype(F32) + self.land(1)[...].astype(F32)

    def drain(self):
        for number in range(6):
            self.one(number).wait_send()


class PlaneGather:
    def __init__(self, me, first, second, send, recv):
        x, y, z, core = me

        def rows(ref, a, b, i):
            return ref.at[a, b, pl.ds(16 * i, 16)]

        self.near = [
            Ring(me, 0, lambda t: first.at[y, t], lambda t, i: rows(first, y, t, i), send.at[0], recv.at[0]),
            Ring(me, 1, lambda t: second.at[x, t], lambda t, i: rows(second, x, t, i), send.at[1], recv.at[1]),
        ]
        self.wide = [
            Ring(me, 1, lambda t: first.at[t], lambda t, i: first.at[t, pl.ds(2 * i, 2)], send.at[2], recv.at[2]),
            Ring(me, 0, lambda t: second.at[t], lambda t, i: second.at[t, pl.ds(2 * i, 2)], send.at[3], recv.at[3]),
        ]

    def start(self):
        for ring in self.near:
            ring.start()

    def relay(self):
        for ring in self.near:
            ring.relay()

    def widen(self):
        for one, two in zip(self.near, self.wide):
            one.finish()
            two.start()

    def relay_wide(self):
        for ring in self.wide:
            ring.relay()

    def finish(self):
        for ring in self.wide:
            ring.finish()

    def drain(self):
        for ring in self.near + self.wide:
            ring.drain()


class PlaneSum:
    def __init__(self, me, first, second, tmp_wide, land_wide, tmp, land, send, recv):
        x, y, z, core = me
        self.place = (y, x)
        self.refs = (first, second)

        def wide(axis, ref, n):
            return RingSum(
                me, axis, lambda t: ref.at[t], lambda t, i: ref.at[t, pl.ds(2 * i, 2)],
                lambda i: tmp_wide.at[n, i], lambda i: land_wide.at[n, i],
                lambda i, j: land_wide.at[n, i, pl.ds(2 * j, 2)], send.at[n], recv.at[n],
            )

        def near(axis, ref, a, n):
            return RingSum(
                me, axis, lambda t: ref.at[a, t], lambda t, i: ref.at[a, t, pl.ds(16 * i, 16)],
                lambda i: tmp.at[n, i], lambda i: land.at[n, i],
                lambda i, j: land.at[n, i, pl.ds(16 * j, 16)], send.at[2 + n], recv.at[2 + n],
            )

        self.wide = [wide(1, first, 0), wide(0, second, 1)]
        self.near = [near(0, first, y, 0), near(1, second, x, 1)]

    def start(self):
        for ring in self.wide:
            ring.start()

    def relay_wide(self):
        for ring in self.wide:
            ring.relay()

    def narrow(self):
        for number in range(2):
            total = self.wide[number].finish()
            self.refs[number][self.place[number]] = total.astype(BF)
            self.near[number].start()

    def relay(self):
        for ring in self.near:
            ring.relay()

    def finish(self):
        return [ring.finish() for ring in self.near]

    def drain(self):
        for ring in self.wide + self.near:
            ring.drain()


def plane_sum_scratch(columns):
    return [
        pltpu.VMEM((2, 2, 2, 32, columns), BF), pltpu.VMEM((2, 2, 4, 32, columns), BF),
        pltpu.VMEM((2, 2, 16, columns), BF), pltpu.VMEM((2, 2, 32, columns), BF),
        pltpu.SemaphoreType.DMA((4, 6)), pltpu.SemaphoreType.DMA((4, 6)),
    ]


class LineGather:
    def __init__(self, me, slots, send, recv, csend, crecv):
        self.me, self.slots, self.csend, self.crecv = me, slots, csend, crecv
        x, y, z, core = me
        half = slots.shape[1] // 2
        self.ring = Ring(
            me, 2, lambda t: slots.at[t * 2 + core],
            lambda t, i: slots.at[t * 2 + core, pl.ds(half * i, half)], send, recv,
        )

    def cross(self, k, mine=True):
        x, y, z, core = self.me
        t = (z + k) % 4
        ref = self.slots.at[t * 2 + (core if mine else 1 - core)]
        return copy(ref, ref, self.csend.at[t], self.crecv.at[t], other_core(self.me))

    def start(self):
        self.ring.start()
        self.cross(0).start()

    def relay(self):
        self.ring.relay()
        self.ring.near()
        self.cross(1).start()
        self.cross(3).start()

    def finish_far(self):
        self.ring.finish()
        self.cross(2).start()

    def wait(self, k):
        self.cross(k, False).wait_recv()

    def drain(self):
        self.ring.drain()
        for k in range(4):
            self.cross(k).wait_send()


def line_gather_sems():
    return [dma(6), dma(6), dma(4), dma(4)]


def dma(*n):
    return pltpu.SemaphoreType.DMA(n) if n else pltpu.SemaphoreType.DMA


class Io:
    def __init__(self, ins, outs, in_sem, out_sem):
        self.ins = [pltpu.make_async_copy(far, near, in_sem.at[n]) for n, (far, near) in enumerate(ins)]
        self.outs = [pltpu.make_async_copy(near, far, out_sem.at[n]) for n, (near, far) in enumerate(outs)]
        self.here = 0
        self.left = []

    def start(self, first, last=None):
        for one in self.ins[first:last]:
            one.start()

    def arrive(self, number=None):
        number = len(self.ins) if number is None else number
        while self.here < number:
            self.ins[self.here].wait()
            self.here += 1

    def leave(self, number):
        self.outs[number].start()
        self.left.append(number)

    def close(self):
        self.arrive()
        for number in range(len(self.outs)):
            if number not in self.left:
                self.leave(number)
        for number in self.left:
            self.outs[number].wait()


def comm_call(kernel, out_shape, scratch, number, *args, far_in=(), far_out=(), scalar_in=(), late=None):
    near_in = [n for n in range(len(args)) if n not in far_in and n not in scalar_in]
    near_out = [n for n in range(len(out_shape)) if n not in far_out]

    def body(*refs):
        ins, refs = list(refs[: len(args)]), refs[len(args) :]
        outs, refs = list(refs[: len(out_shape)]), refs[len(out_shape) :]
        near = refs[: len(near_in) + len(near_out)]
        rest, sems = refs[len(near) : -2], refs[-2:]
        io = Io(
            [(ins[n], near[i]) for i, n in enumerate(near_in)],
            [(near[len(near_in) + i], outs[n]) for i, n in enumerate(near_out)],
            *sems,
        )
        io.start(0, late)
        for i, n in enumerate(near_in):
            ins[n] = near[i]
        for i, n in enumerate(near_out):
            outs[n] = near[len(near_in) + i]
        kernel(io, *ins, *outs, *rest)
        io.close()

    spaces = [pltpu.VMEM(args[n].shape, args[n].dtype) for n in near_in]
    spaces += [pltpu.VMEM(out_shape[n].shape, out_shape[n].dtype) for n in near_out]
    if number is None:
        params = pltpu.CompilerParams(vmem_limit_bytes=VMEM_LIMIT)
    else:
        params = pltpu.CompilerParams(
            collective_id=number, has_side_effects=True, vmem_limit_bytes=VMEM_LIMIT
        )
    return pl.pallas_call(
        body,
        out_shape=out_shape,
        in_specs=[pl.BlockSpec(memory_space=pltpu.SMEM if n in scalar_in else pl.ANY) for n in range(len(args))],
        out_specs=tuple(pl.BlockSpec(memory_space=pl.ANY) for _ in out_shape),
        scratch_shapes=[*spaces, *scratch, dma(max(len(near_in), 1)), dma(max(len(near_out), 1))],
        compiler_params=params,
    )(*args)


def shape(*dims, dtype=BF):
    return jax.ShapeDtypeStruct(dims, dtype)


def scale_of(rows):
    return lax.rsqrt(jnp.sum(rows * rows, axis=-1, keepdims=True) * (1.0 / D) + EPS_NORM)


def norm_back(grad, rows, scale, gain):
    weighted = grad * gain
    mean = jnp.sum(weighted * rows, axis=-1, keepdims=True) * (1.0 / D)
    return scale * weighted - rows * (scale * scale * scale * mean), jnp.sum(grad * rows * scale, axis=0)


def dot(left, right):
    return jnp.dot(left, right, preferred_element_type=F32)


def dot_tn(left, right):
    return lax.dot_general(left, right, (((0,), (0,)), ((), ())), preferred_element_type=F32)


def dot_nt(left, right):
    return lax.dot_general(left, right, (((1,), (1,)), ((), ())), preferred_element_type=F32)


def lane(rows):
    return lax.broadcasted_iota(jnp.int32, (rows, 128), 1)


def swap_halves(value):
    low = lane(value.shape[0]) % HD < HD // 2
    return jnp.where(low, pltpu.roll(value, 128 - HD // 2, 1), pltpu.roll(value, HD // 2, 1))


def rope(value, cos, sin):
    return value * cos + swap_halves(value) * sin


def side_of(value, side):
    return jnp.where(lane(value.shape[0]) // HD == side, value, 0.0)


def moved(value, source, target):
    shifted = value if source == target else pltpu.roll(value, HD, 1)
    return side_of(shifted, target)


def local_copy(src, dst, sem):
    return pltpu.make_async_copy(src, dst, sem)


def piece_code(piece):
    later = piece - PROMPT // PIECE
    tail = 4096 * (later // (CONT // PIECE) + 1) + PROMPT + later % (CONT // PIECE) * PIECE
    return jnp.where(later < 0, piece * PIECE, tail)


def forward_kernel(
    io, layout, wq, wk, wv, wvec, wo, spread, wg, wu, wd, tok, cot, turns, pick, spots, holds,
    h_out, n2_out, o_nat, invp, o_low, vec, cos, sin, n1_s, x_s, dy_s, q_ext, keys, values, wa, wb, wdn, wf, dyg, p_far,
    msg, land, msg_b, land_b, w8, pk, s_a, s_b, k_s, v_s, o_ext, p_a, p_b, marks,
    s1s, s1r, s2s, s2r, dns, dnr, fs, fr, as_, ar, bs, br, ls, lr, lcs, lcr, cs, cr, kps, kpr, kxs, kxr, vps, vpr, vxs, vxr, own_sem, p_sem,
):
    me = place()
    x, y, z, core = me
    p = z * 2 + core
    low = y % 2
    greet(line_targets(me) + ring_targets(me, x_peer) + ring_targets(me, y_peer))
    io.arrive(4)

    firsts = []

    def hand_round(out, arrived, send, recv):
        for k in range(1, 8):
            t, target = line_peer(me, k)
            one = copy(out.at[t], arrived.at[p], send.at[k], recv.at[p], target)
            one.start()
            firsts.append(one)
        arrived[p] = out[p]

    def collect(out, arrived, send, recv):
        for k in range(1, 8):
            t, target = line_peer(me, k)
            copy(out.at[t], arrived.at[t], send.at[k], recv.at[t], target).wait_recv()

    def folded(whole, columns):
        return jnp.concatenate([whole[:, :columns], whole[:, columns:]], axis=0).astype(BF)

    def unfolded(arrived, j):
        a = arrived[2 * j].astype(F32)
        b = arrived[2 * j + 1].astype(F32)
        return jnp.concatenate([jnp.concatenate([a[:8], b[:8]], 0), jnp.concatenate([a[8:], b[8:]], 0)], 1).astype(BF)

    def blank(columns):
        return jnp.zeros((8, columns), F32)

    w8[...] = jnp.zeros_like(w8)
    first = 0
    for ref in (wq, wk, wv):
        w8[0:7, first : first + ref.shape[1]] = ref[...]
        first += ref.shape[1]
    w8[7:8, 0:NVEC] = wvec[...]
    halves = (
        folded(jnp.concatenate([w8[:, 0:A1], blank(128)], 1), 384),
        folded(jnp.concatenate([w8[:, A1:QKV], blank(256)], 1), 384),
    )
    for t in range(8):
        msg[t] = halves[t % 2]
    hand_round(msg, land, s1s, s1r)
    io.arrive(9)
    w8[0:7, QKV : QKV + DP] = dot(wo[...].astype(BF), spread[...])
    for n, ref in enumerate((wg, wu, wd)):
        w8[0:7, QKV + DP + FF * n : QKV + DP + FF * (n + 1)] = ref[...]
    for t in range(8):
        base = QKV + DP + FB * t if t < 6 else QKV + DP + FB * 6 + 512 * (t - 6)
        width = FB if t < 6 else 512
        at = QKV + A2 * (t % 2)
        pieces = [w8[:, at : at + A2]]
        for n in range(3):
            pieces.append(w8[:, base + FF * n : base + FF * n + width])
            if width < FB:
                pieces.append(blank(FB - width))
        pieces.append(blank(128))
        msg_b[t] = folded(jnp.concatenate(pieces, axis=1), 1280)
    hand_round(msg_b, land_b, s2s, s2r)
    io.arrive()
    x_s[...] = dot(tok[...], spread[...])
    io.leave(9)
    dy_s[...] = dot(cot[...], spread[...]).astype(BF)
    io.leave(10)
    own_dy = local_copy(dy_s, dyg.at[p], own_sem.at[2])
    own_dy.start()
    collect(msg, land, s1s, s1r)
    for j in range(4):
        rows = slice(16 * (j % 2), 16 * (j % 2) + 16)
        at = (y, x) if j < 2 else (x, y)
        wa[core, j // 2, at[0], at[1], rows, :] = unfolded(land, j)[:, 0:A1]
    att = PlaneGather(me, wa.at[core, 0], wa.at[core, 1], as_, ar)
    out = PlaneGather(me, wb.at[core, 0], wb.at[core, 1], bs, br)
    ffn = PlaneGather(me, wf.at[0], wf.at[1], fs, fr)
    down = [
        Ring(me, n, lambda t, n=n: None, lambda t, i, n=n: wdn.at[n, t, pl.ds(16 * i, 16)], dns.at[n], dnr.at[n])
        for n in range(2)
    ]
    line = LineGather(me, dyg, ls, lr, lcs, lcr)
    att.start()
    codes = jnp.zeros((1, 128), jnp.int32)
    for t in range(32):
        block = t // 4
        code = piece_code(layout[0, (block % 2 * 4 + block // 2) * 4 + t % 4])
        codes = jnp.where(lane(1) % HD == t, code, codes)
    sign = jnp.where(lane(PIECE) % HD < HD // 2, -1.0, 1.0)
    for i in range(4):
        code = piece_code(layout[0, 4 * (low * 4 + x) + i])
        rows = slice(PIECE * i, PIECE * i + PIECE)
        seen = (codes <= code) & ((codes < PROMPT) | (codes >= code // 4096 * 4096))
        barred = jnp.where((lane(1) % HD < 32) & jnp.logical_not(seen), MASKED, 0.0)
        marks[rows, :] = jnp.zeros((PIECE, 128), F32) + barred
        number = code % 4096 // PIECE
        cos_far, sin_far = turns[0, pl.ds(number, 1), :], turns[1, pl.ds(number, 1), :]
        cos_near, sin_near = turns[2, 0:PIECE, :], turns[3, 0:PIECE, :]
        cos[rows, :] = cos_far * cos_near - sin_far * sin_near
        sin[rows, :] = (sin_far * cos_near + cos_far * sin_near) * sign
    io.leave(6)
    io.leave(7)
    att.relay()
    own_dy.wait()
    line.start()
    att.widen()
    collect(msg_b, land_b, s2s, s2r)
    for j in range(4):
        rows = slice(16 * (j % 2), 16 * (j % 2) + 16)
        at = (y, x) if j < 2 else (x, y)
        block = unfolded(land_b, j)
        wb[core, j // 2, at[0], at[1], rows, :] = block[:, 0:A2]
        pk[j // 2, rows, :] = block[:, A2 : A2 + 2 * FB]
        wdn[j // 2, (x, y)[j // 2], rows, :] = block[:, A2 + 2 * FB : A2 + FFN]
    out.start()
    owns = [
        local_copy(pk.at[0], wf.at[0, y, x], own_sem.at[0]), local_copy(pk.at[1], wf.at[1, x, y], own_sem.at[1])
    ]
    for one in owns:
        one.start()
    att.relay_wide()
    out.relay()
    for one in owns:
        one.wait()
    ffn.start()
    att.finish()
    cross = [
        copy(ref.at[core], ref.at[core], cs.at[n], cr.at[n], other_core(me)) for n, ref in enumerate((wa, wb))
    ]
    crossed = [
        copy(ref.at[1 - core], ref.at[1 - core], cs.at[n], cr.at[n], other_core(me)) for n, ref in enumerate((wa, wb))
    ]
    cross[0].start()
    out.widen()
    crossed[0].wait_recv()

    table = dot(pick[...], wide(wa, 0, 0, 128)).astype(BF)
    vec[...] = jnp.sum(dot(table, spots[...]) * holds[...].astype(F32), axis=0, keepdims=True)
    xs = x_s[...]
    n1_s[...] = (xs * scale_of(xs) * vec[:, 0:DP]).astype(BF)
    second = dot(n1_s[...], wide(wa, 1, 0, QKV - A1)) + vec[:, 2 * DP + A1 :]
    kv_pre = second[:, D - A1 :]
    keys[x, low] = rope(kv_pre[:, 0:128], cos[...], sin[...]).astype(BF)
    values[x, low] = kv_pre[:, 128:256].astype(BF)
    key_pair = copy(keys.at[x, low], keys.at[x, low], kps, kpr, pair_peer(me))
    key_pair.start()
    key_ring = Ring(me, 0, lambda t: keys.at[t], lambda t, i: keys.at[t, i], kxs, kxr)
    value_ring = Ring(
        me, 0, lambda t: values.at[t, low], lambda t, i: values.at[t, low, pl.ds(128 * i, 128)], vxs, vxr
    )
    value_ring.start()
    value_pair = copy(values.at[:, low], values.at[:, low], vps, vpr, pair_peer(me))
    io.leave(5)
    io.leave(8)
    io.leave(14)
    q_pre = jnp.concatenate(
        [dot(n1_s[...], wide(wa, 0, 0, A1)) + vec[:, 2 * DP : 2 * DP + A1], second[:, : D - A1]], axis=1
    )
    copy(keys.at[x, 1 - low], keys.at[x, 1 - low], kps, kpr, pair_peer(me)).wait_recv()
    key_ring.start()
    value_ring.relay()
    for head in range(HEADS):
        block = q_pre[:, 128 * (head // 2) : 128 * (head // 2) + 128]
        turned = rope(block, cos[...], sin[...]) * (HD**-0.5 * LOG_E)
        turned = moved(turned, head % 2, head // 7)
        q_ext[head] = (turned + side_of(marks[...], 1 - head // 7)).astype(BF)
    io.leave(11)
    value_ring.finish()
    value_pair.start()
    key_ring.relay()
    out.relay_wide()
    ffn.relay()
    ffn.widen()
    line.relay()
    key_ring.finish()
    io.leave(12)
    out.finish()
    cross[1].start()
    for ring in down:
        ring.start()
    all_keys = keys[...].reshape(8 * TOK, 128).astype(F32)
    piece = lax.broadcasted_iota(jnp.int32, (8 * TOK, 128), 0) // PIECE
    marked = jnp.where(lane(8 * TOK) % HD == piece, 1.0, 0.0)
    for j in range(2):
        k_s[j] = jnp.where(lane(8 * TOK) // HD == j, all_keys, marked).astype(BF)
    apart = lax.broadcasted_iota(jnp.int32, (TOK, TOK), 1) - lax.broadcasted_iota(jnp.int32, (TOK, TOK), 0)
    same = lax.broadcasted_iota(jnp.int32, (TOK, TOK), 1) // PIECE == lax.broadcasted_iota(jnp.int32, (TOK, TOK), 0) // PIECE
    diagonal = pl.ds(pl.multiple_of((x * 2 + low) * TOK, TOK), TOK)
    copy(values.at[:, 1 - low], values.at[:, 1 - low], vps, vpr, pair_peer(me)).wait_recv()
    io.leave(13)
    v_s[:, 0:128] = values[...].reshape(8 * TOK, 128)
    v_s[:, 128:256] = jnp.ones((8 * TOK, 128), BF)
    invp[...] = jnp.zeros_like(invp)

    p_s = (p_a, p_b)
    s_s = (s_a, s_b)

    def put(i, j):
        return local_copy(p_s[j].at[i % 2], p_far.at[7 * j + i], p_sem.at[j, i % 2])

    def attend(i, carry):
        @pl.when(i >= 2)
        def _():
            for j in range(2):
                put(i, j).wait()

        for j in range(2):
            s_s[j][...] = dot_nt(q_ext[7 * j + i], k_s[j])
        inverse_all = invp[...]
        for j in range(2):
            s_s[j][:, diagonal] = jnp.where(same & (apart > 0), MASKED, s_s[j][:, diagonal])
            scores = s_s[j][...]
            numerators = jnp.exp2(scores - jnp.max(scores, axis=1, keepdims=True)).astype(BF)
            p_s[j][i % 2] = numerators
            both = dot(numerators, v_s[...])
            inverse = 1.0 / both[:, 128:256]
            o_ext[7 * j + i] = side_of(both[:, 0:128] * inverse, j)
            inverse_all = jnp.where(lane(TOK) == 7 * j + i, inverse, inverse_all)
        invp[...] = inverse_all
        for j in range(2):
            put(i, j).start()
        return carry

    lax.fori_loop(0, 4, attend, 0)
    crossed[1].wait_recv()
    io.leave(15)
    ffn.relay_wide()
    for ring in down:
        ring.relay()
    line.finish_far()
    lax.fori_loop(4, 7, attend, 0)
    for block in range(7):
        pieces = [moved(o_ext[2 * block + e], (2 * block + e) // 7, e) for e in range(2)]
        o_nat[:, 128 * block : 128 * block + 128] = pieces[0] + pieces[1]

    o_low[...] = dot(o_nat[...].astype(BF), spread[...]).astype(BF)
    for n in range(2):
        cols = slice(A2 * n, A2 * n + A2)
        h_out[:, cols] = x_s[:, cols] + dot(o_low[...], wide(wb, n, 0, A2))
    h = h_out[...]
    n2_out[...] = (h * scale_of(h) * vec[:, DP : 2 * DP]).astype(BF)
    for number in range(5):
        io.leave(number)
    for ring in down:
        ring.finish()
    io.leave(16)
    ffn.finish()
    for k in range(4):
        line.wait(k)
    for i in (5, 6):
        for j in range(2):
            put(i, j).wait()
    line.drain()
    att.drain()
    out.drain()
    ffn.drain()
    for ring in down:
        ring.drain()
    key_ring.drain()
    value_ring.drain()
    key_pair.wait_send()
    value_pair.wait_send()
    for one in firsts + cross:
        one.wait_send()


def wide(ref, side, first, columns):
    return ref[side, :, :, :, :, first : first + columns].reshape(DP, columns)


def forward(*args):
    row = pltpu.VMEM
    return comm_call(
        forward_kernel,
        (
            shape(TOK, DP, dtype=F32), shape(TOK, DP), shape(TOK, D, dtype=F32), shape(TOK, 128, dtype=F32),
            shape(TOK, DP), shape(1, LANES, dtype=F32), shape(TOK, 128, dtype=F32), shape(TOK, 128, dtype=F32),
            shape(TOK, DP), shape(TOK, DP, dtype=F32), shape(TOK, DP), shape(HEADS, TOK, 128),
            shape(4, 2, TOK, 128), shape(4, 2, TOK, 128),
            shape(2, 2, 4, 4, 32, A1), shape(2, 2, 4, 4, 32, A2), shape(2, 4, 32, FB), shape(2, 4, 4, 32, 2 * FB),
            shape(8, TOK, DP), shape(HEADS, TOK, 8 * TOK),
        ),
        [
            row((8, 16, 384), BF), row((8, 16, 384), BF), row((8, 16, 1280), BF), row((8, 16, 1280), BF),
            row((8, QKV + DP + 3 * FF), F32), row((2, 32, 2 * FB), BF), row((TOK, 8 * TOK), F32),
            row((TOK, 8 * TOK), F32), row((2, 8 * TOK, 128), BF), row((8 * TOK, 256), BF),
            row((HEADS, TOK, 128), F32), row((2, TOK, 8 * TOK), BF), row((2, TOK, 8 * TOK), BF),
            row((TOK, 128), F32),
            dma(8), dma(8), dma(8), dma(8), dma(2, 6), dma(2, 6), dma(4, 6), dma(4, 6), dma(4, 6), dma(4, 6), dma(4, 6), dma(4, 6),
            *line_gather_sems(), dma(2), dma(2), dma(), dma(), dma(6), dma(6), dma(), dma(), dma(6), dma(6),
            dma(3), dma(2, 2),
        ],
        1, *args, far_out=(17, 18, 19), scalar_in=(0,),
    )


def ffn_kernel(
    io, n2, wf, dyg, wdn, dn2_out, reduced, y_far, g_far,
    wd, grads, grads_d, n2g, dparts, yparts, got, tmp, land, hid_all, dgu_all, dhid_all, gu_s,
    f_tw, f_lw, f_t, f_l, f_s, f_r, leave, wds, wdr, ls, lr, lcs, lcr, gs, gr, ds, dr,
):
    me = place()
    x, y, z, core = me
    rows = [
        pltpu.make_async_copy(wdn.at[0], wd.at[0, y], leave.at[0]),
        pltpu.make_async_copy(wdn.at[1], wd.at[1, x], leave.at[1]),
    ]
    for one in rows:
        one.start()
    greet(ring_targets(me, z_peer) + [other_core(me)] + ring_targets(me, x_peer) + ring_targets(me, y_peer))
    io.arrive(1)
    n2g[z * 2 + core] = n2[...]
    line = LineGather(me, n2g, ls, lr, lcs, lcr)
    line.start()
    for one in rows:
        one.wait()
    gathers = [
        Ring(
            me, 1 - n, lambda t: None, lambda t, i, n=n: wd.at[n, t, pl.ds(2 * i, 2)], wds.at[n], wdr.at[n]
        )
        for n in range(2)
    ]
    for ring in gathers:
        ring.start()

    def both():
        return wf[...].reshape(DP, 2 * FB)

    def down():
        return wd[...].reshape(DP, FB)

    def slot(k, side):
        return (z + k) % 4 * 2 + side

    def one(s, gu=None):
        gu = dot(n2g[s], both()) if gu is None else gu
        gate, up = gu[:, :FB], gu[:, FB:]
        sig = 1.0 / (1.0 + jnp.exp(-gate))
        act = gate * sig
        hid_all[s] = (act * up).astype(BF)
        dhid = dhid_all[s]
        dgu_all[s, :, :FB] = (dhid * up * (sig + act * (1.0 - sig))).astype(BF)
        dgu_all[s, :, FB:] = (dhid * act).astype(BF)
        dparts[s] = dot_nt(dgu_all[s], both()).astype(BF)

    def pair(n, ref, k):
        t = (z + k) % 4
        return copy(ref.at[t * 2 + 1 - core], got.at[n, t], gs.at[n, t], gr.at[n, t], other_core(me))

    def join(n, ref, k):
        t = (z + k) % 4
        pair(n, ref, k).wait_recv()
        add_into(ref.at[t * 2 + core], got.at[n, t])

    def compute(k, between=None):
        if between is None:

            def body(i, carry):
                side = (1 - core) * (1 - i) + core * i
                one(slot(k, side), gu_s[side] if k == 0 else None)
                return carry

            lax.fori_loop(0, 2, body, 0)
        else:
            lax.fori_loop(0, 1, lambda i, carry: (one(slot(k, 1 - core)), carry)[1], 0)
            between()
            lax.fori_loop(0, 1, lambda i, carry: (one(slot(k, core)), carry)[1], 0)
        pair(0, dparts, k).start()

    dsum = RingSum(
        me, 2, lambda t: dparts.at[t * 2 + core], lambda t, i: dparts.at[t * 2 + core, pl.ds(128 * i, 128)],
        lambda i: tmp.at[i], lambda i: land.at[i], lambda i, j: land.at[i, pl.ds(128 * j, 128)], ds, dr,
    )

    def after_first():
        join(0, dparts, 1)
        dsum.one(2).start()

    def after_far():
        join(0, dparts, 2)
        dsum.start_far()

    def hidden_grads(first, last):
        def body(i, carry):
            s = (z * 2 + i) % 8
            dhid_all[s] = dot(dyg[s], down())
            return carry

        lax.fori_loop(first, last, body, 0)

    def own_gates(side, carry):
        gu_s[side] = dot(n2g[z * 2 + side], both())
        return carry

    io.arrive()
    line.wait(0)
    lax.fori_loop(0, 2, own_gates, 0)
    for ring in gathers:
        ring.relay()
    for ring in gathers:
        ring.finish()
    hidden_grads(0, 2)
    compute(0)
    hidden_grads(2, 8)
    line.relay()
    line.wait(1)
    line.wait(3)
    compute(1)
    join(0, dparts, 0)
    line.finish_far()
    line.wait(2)
    compute(2, after_first)
    compute(3, after_far)

    fsum = PlaneSum(me, grads.at[0], grads.at[1], f_tw, f_lw, f_t, f_l, f_s, f_r)
    leaves = []

    def weight_grads(left, right, into, width, first, last):
        for m in range(first, last):
            rows = left[:, :, 256 * m : 256 * m + 256].reshape(8 * TOK, 256)
            value = dot_tn(rows, right[...].reshape(8 * TOK, width)).astype(BF)
            into[m // 2, 2 * (m % 2) : 2 * (m % 2) + 2] = value.reshape(2, 4, 32, width)

    def outputs(k, carry):
        for side in range(2):
            yparts[slot(k, side)] = dot_nt(hid_all[slot(k, side)], down()).astype(BF)
        return carry

    weight_grads(n2g, dgu_all, grads, 2 * FB, 0, 1)
    join(0, dparts, 3)
    dsum.one(3).start()
    weight_grads(n2g, dgu_all, grads, 2 * FB, 1, 2)
    fsum.wide[0].start()
    weight_grads(n2g, dgu_all, grads, 2 * FB, 2, 4)
    fsum.wide[1].start()
    dsum.relay()
    weight_grads(dyg, hid_all, grads_d, FB, 0, 4)
    leaves.append(pltpu.make_async_copy(grads_d, g_far, leave.at[4]))
    leaves[0].start()
    fsum.wide[0].relay()
    lax.fori_loop(0, 2, outputs, 0)
    for k in range(2):
        pair(1, yparts, k).start()
    fsum.wide[1].relay()
    dn2_out[...] = dsum.finish()
    io.leave(0)
    lax.fori_loop(2, 4, outputs, 0)
    for k in range(2, 4):
        pair(1, yparts, k).start()
    for k in range(4):
        join(1, yparts, k)
        t = (z + k) % 4
        one_out = pltpu.make_async_copy(yparts.at[t * 2 + core], y_far.at[t], leave.at[k])
        one_out.start()
        leaves.append(one_out)
    for n in range(2):
        reduced[n] = fsum.wide[n].finish().astype(BF)
    io.leave(1)
    for ring in fsum.wide + gathers:
        ring.drain()
    line.drain()
    for n, ref in enumerate((dparts, yparts)):
        for k in range(4):
            pair(n, ref, k).wait_send()
    dsum.drain()
    for one_out in leaves:
        one_out.wait()


def feed_forward(n2, wf, dyg, wdn):
    slots = pltpu.VMEM((8, TOK, DP), BF)
    return comm_call(
        ffn_kernel,
        (shape(TOK, DP, dtype=F32), shape(2, 4, 32, 2 * FB), shape(4, TOK, DP), shape(2, 4, 4, 32, FB)),
        [
            pltpu.VMEM((2, 4, 4, 32, FB), BF), pltpu.VMEM((2, 4, 4, 32, 2 * FB), BF), pltpu.VMEM((2, 4, 4, 32, FB), BF),
            slots, slots, slots, pltpu.VMEM((2, 4, TOK, DP), BF),
            pltpu.VMEM((2, TOK // 2, DP), BF), pltpu.VMEM((2, TOK, DP), BF),
            pltpu.VMEM((8, TOK, FB), BF), pltpu.VMEM((8, TOK, 2 * FB), BF), pltpu.VMEM((8, TOK, FB), F32),
            pltpu.VMEM((2, TOK, 2 * FB), F32),
            *plane_sum_scratch(2 * FB), dma(6), dma(2, 6), dma(2, 6),
            *line_gather_sems(), dma(2, 4), dma(2, 4), dma(6), dma(6),
        ],
        2, n2, wf, dyg, wdn, far_in=(3,), far_out=(2, 3),
    )


def plane_peer(me, k):
    x, y, z, core = me
    t = (y * 4 + x + k) % 16
    return t, device(t % 4, t // 4, z, core)


def fold_squares(value):
    total = jnp.zeros((8, 128), F32)
    for b in range(value.shape[1] // 128):
        piece = value[:, 128 * b : 128 * b + 128]
        total = total + piece * piece
    return total


def backward_kernel(
    io, reduced, own, yb, dn2, h, dy, vec, o_low, wb, spread, invp, o_nat, q_ext, k_s, v_in,
    n1, xs, wa, cos, sin, spots, holds, p_far,
    result, input_grad, grads, att_grads, norm,
    ytmp, yland, ag0, ag1, got0, got1, bland, ent, eland, asums, aland, sums, squares, lsq, psq,
    v_s, do_s, do_ext, do_t, q_t, dq_ext, dkt, dvt, p_s, ds_s, kvp, kvtmp, kvland, give, take, dh, dqkv, dn1,
    n_t, n_l, n_s, n_r, f_tw, f_lw, f_t, f_l, f_s, f_r, a_tw, a_lw, a_t, a_l, a_s, a_r,
    p_sem, bs, br, es, er, ys, yr, cs, cr, ks, kr, kps, kpr, lfs, lfr, las, lar, qs, qr, ts, tr,
):
    me = place()
    x, y, z, core = me
    p = z * 2 + core
    q = y * 4 + x
    low = y % 2

    units = [(0, 2), (2, 2), (4, 2), (6, 1), (7, 2), (9, 2), (11, 2), (13, 1)]

    def get(unit):
        head, count = units[unit]
        rows = pl.ds(0, count)
        return local_copy(p_far.at[pl.ds(head, count)], p_s.at[unit % 2, rows], p_sem.at[unit % 2])

    for unit in range(2):
        get(unit).start()
    io.start(15)
    greet(line_targets(me) + [plane_peer(me, k)[1] for k in range(1, 16)])
    io.arrive(3)
    fsum = PlaneSum(me, own.at[0], own.at[1], f_tw, f_lw, f_t, f_l, f_s, f_r)
    asum = PlaneSum(me, got0.at[0], got0.at[1], a_tw, a_lw, a_t, a_l, a_s, a_r)

    def send_narrow():
        for k in range(1, 16):
            t, target = plane_peer(me, k)
            copy(got1.at[t], bland.at[q], bs.at[k], br.at[q], target).start()
        bland[q] = got1[q]

    def by_place(value):
        for t in range(16):
            turned = t % 4 * 4 + t // 4
            yield t, value[32 * t : 32 * t + 32], value[512 + 32 * turned : 544 + 32 * turned]

    ysum = RingSum(
        me, 2, lambda t: yb.at[t], lambda t, i: yb.at[t, pl.ds(128 * i, 128)],
        lambda i: ytmp.at[i], lambda i: yland.at[i], lambda i, j: yland.at[i, pl.ds(128 * j, 128)], ys, yr,
    )
    nears = [
        RingSum(
            me, n, lambda t, n=n: reduced.at[n, t], lambda t, i, n=n: reduced.at[n, t, pl.ds(16 * i, 16)],
            lambda i, n=n: n_t.at[n, i], lambda i, n=n: n_l.at[n, i],
            lambda i, j, n=n: n_l.at[n, i, pl.ds(16 * j, 16)], n_s.at[n], n_r.at[n],
        )
        for n in range(2)
    ]
    for ring in nears:
        ring.start()
    fsum.start()
    ysum.start()

    io.arrive(10)
    scale_two = scale_of(h[...])
    dh_part, dgain_two = norm_back(dn2[...], h[...], scale_two, vec[:, DP : 2 * DP])
    dh[...] = dy[...].astype(F32) + dh_part
    da = dh[...].astype(BF)
    dwo = dot_tn(o_low[...], da).astype(BF)
    ag0[...] = dwo[:, 0:D].reshape(2, 4, 4, 32, D)
    ag1[...] = jnp.zeros_like(ag1)
    for t, one, two in by_place(dwo[:, D:DP]):
        ag1[t, 0:32, 0:128] = one
        ag1[t, 32:64, 0:128] = two

    def give_part(n, number):
        return copy((ag0, ag1)[n], (got0, got1)[n], cs.at[number, n], cr.at[number, n], other_core(me))

    @pl.when(core == 0)
    def _():
        give_part(0, 0).start()
        give_part(1, 0).start()

    do_far = (dot_nt(da[:, 0:A2], wide(wb, 0, 0, A2)) + dot_nt(da[:, A2:DP], wide(wb, 1, 0, A2))).astype(BF)
    do_s[...] = dot_nt(do_far, spread[...]).astype(BF)
    io.arrive(15)
    all_values = v_in[...].reshape(8 * TOK, 128).astype(F32)
    for j in range(2):
        ones = jnp.where(lane(8 * TOK) % HD < 3, 1.0, 0.0)
        v_s[j] = jnp.where(lane(8 * TOK) // HD == j, all_values, ones).astype(BF)

    def prepare(unit):
        first, count = units[unit]
        for spot in range(count):
            head = first + spot
            j = head // 7
            lanes = slice(128 * (head // 2), 128 * (head // 2) + 128)
            inverse = invp[:, head : head + 1]
            block = side_of(do_s[:, lanes].astype(F32), head % 2)
            rest = -jnp.sum(block * o_nat[:, lanes], axis=1, keepdims=True) * inverse
            value = moved(block * inverse, head % 2, j)
            for n in range(3):
                part = rest.astype(BF).astype(F32)
                value = jnp.where(lane(TOK) == HD * (1 - j) + n, part, value)
                rest = rest - part
            do_ext[head] = value.astype(BF)
            columns = slice(TOK * spot, TOK * spot + TOK)
            do_t[unit, :, columns] = value.T[HD * j : HD * j + HD].astype(BF)
            q_t[unit, :, columns] = q_ext[head].astype(F32).T[HD * j : HD * j + HD].astype(BF)

    for ring in nears:
        ring.relay()
    prepare(0)
    dkt[...] = jnp.zeros_like(dkt)
    dvt[...] = jnp.zeros_like(dvt)

    @pl.when(core == 1)
    def _():
        give_part(0, 0).wait_recv()
        add_into(got0, ag0)
        asum.start()
        give_part(1, 0).wait_recv()
        add_into(got1, ag1)
        send_narrow()

    def heads(unit):
        head, count = units[unit]
        j = head // 7
        half = slice(HD * j, HD * j + HD)
        rows = count * TOK
        base = 2 * TOK if unit == 7 else 0
        get(unit).wait()
        dp = dot_nt(do_ext[head : head + count].reshape(rows, 128), v_s[j])
        numerators = p_s[unit % 2, 0:count].reshape(rows, 8 * TOK)
        dvt[half, :] += dot(do_t[unit, :, 0:rows], numerators)
        ds_s[base : base + rows, :] = dp.astype(BF) * numerators
        if unit + 1 < len(units):
            prepare(unit + 1)
        dkt[half, :] += dot(q_t[unit, :, 0:rows], ds_s[base : base + rows, :])
        if unit < 6:
            query_grads(head, count)
        if unit + 2 < len(units):
            get(unit + 2).start()

    def query_grads(head, count):
        value = dot(ds_s[0 : count * TOK, :], k_s[...].reshape(8 * TOK, 128))
        dq_ext[head : head + count] = value.reshape(count, TOK, 128)

    def kv_sum(j):
        return RingSum(
            me, 0, lambda t: kvp.at[j, t], lambda t, i: kvp.at[j, t, i],
            lambda i: kvtmp.at[j, i], lambda i: kvland.at[j, i], lambda i, n: kvland.at[j, i, n],
            ks.at[j], kr.at[j],
        )

    def kv_pack(j):
        for t in range(8):
            lanes = slice(256 * t, 256 * t + 256)
            kvp[j, t // 2, t % 2, 0:HD, :] = (dkt[HD * j : HD * j + HD, lanes] * (1.0 / LOG_E)).astype(BF)
            kvp[j, t // 2, t % 2, HD:128, :] = dvt[HD * j : HD * j + HD, lanes].astype(BF)

    def kv_pair(j):
        return copy(give.at[j, 1 - low], take.at[j], kps.at[j], kpr.at[j], pair_peer(me))

    def kv_cross(j):
        give[j] = kv_sums[j].finish().astype(BF)
        kv_pair(j).start()

    def kv_total(j):
        kv_pair(j).wait_recv()
        return give[j, low].astype(F32) + take[j].astype(F32)

    kv_sums = [kv_sum(0), kv_sum(1)]
    heads(0)
    heads(1)
    fsum.relay_wide()
    ysum.relay()

    @pl.when(core == 1)
    def _():
        asum.relay_wide()

    heads(2)
    heads(3)
    kv_pack(0)
    kv_sums[0].start()
    fsum.narrow()

    @pl.when(core == 1)
    def _():
        asum.narrow()

    heads(4)
    heads(5)
    kv_sums[0].relay()
    fsum.relay()

    @pl.when(core == 1)
    def _():
        asum.relay()

    heads(6)
    kv_cross(0)
    heads(7)
    kv_pack(1)
    kv_sums[1].start()

    query_grads(11, 3)
    io.arrive()
    for block in range(7):
        pieces = [moved(dq_ext[2 * block + e], (2 * block + e) // 7, e) for e in range(2)]
        turned = rope((pieces[0] + pieces[1]) * HD**-0.5, cos[...], -sin[...])
        dqkv[:, 128 * block : 128 * block + 128] = turned.astype(BF)
    @pl.when(core == 0)
    def _():
        give_part(0, 0).wait_send()
        give_part(1, 0).wait_send()

    ag0[...] = dot_tn(n1[...], dqkv[:, 0:D]).astype(BF).reshape(2, 4, 4, 32, D)

    @pl.when(core == 1)
    def _():
        give_part(0, 1).start()

    kv_sums[1].relay()
    dn1[...] = dot_nt(dqkv[:, 0:A1], wide(wa, 0, 0, A1)) + dot_nt(dqkv[:, A1:D], wide(wa, 1, 0, D - A1))
    kv_cross(1)

    @pl.when(core == 0)
    def _():
        give_part(0, 1).wait_recv()
        add_into(got0, ag0)
        asum.start()

    dkv = [kv_total(0), kv_total(1)]
    dk = jnp.concatenate([dkv[0][0:HD], dkv[1][0:HD]], axis=0).T
    dv = jnp.concatenate([dkv[0][HD:128], dkv[1][HD:128]], axis=0).T
    dqkv[:, D : D + 128] = rope(dk, cos[...], -sin[...]).astype(BF)
    dqkv[:, D + 128 : QKV] = dv.astype(BF)
    for t, one, two in by_place(dot_tn(n1[...], dqkv[:, D:QKV]).astype(BF)):
        ag1[t, 0:32] = one
        ag1[t, 32:64] = two

    @pl.when(core == 1)
    def _():
        give_part(1, 1).start()

    @pl.when(core == 0)
    def _():
        asum.relay_wide()
        give_part(1, 1).wait_recv()
        add_into(got1, ag1)
        send_narrow()

    dn1_all = dn1[...] + dot_nt(dqkv[:, D:QKV], wide(wa, 1, D - A1, QKV - D))
    scale_one = scale_of(xs[...])
    dx_part, dgain_one = norm_back(dn1_all, xs[...], scale_one, vec[:, 0:DP])
    dbias = jnp.sum(dqkv[...].astype(F32), axis=0, keepdims=True)
    dvec = jnp.concatenate([dgain_one[None], dgain_two[None], dbias], axis=1)
    dvec_high = dvec.astype(BF).astype(F32)
    entries = jnp.zeros((128, 128), F32)
    for part in (dvec_high, dvec - dvec_high):
        entries = entries + dot_nt((holds[...].astype(F32) * part).astype(BF), spots[...])
    ent[...] = entries.reshape(16, 8, 128)
    sent = []
    for k in range(1, 16):
        t, target = plane_peer(me, k)
        one = copy(ent.at[t], eland.at[q], es.at[k], er.at[q], target)
        one.start()
        sent.append(one)
    eland[q] = ent[q]

    @pl.when(core == 0)
    def _():
        asum.narrow()

    sum_f = fsum.finish()
    for i in range(2):
        sums[4 * i : 4 * i + 4, :, 0 : 2 * FB] = nears[i].finish().reshape(4, 8, 2 * FB)
        sums[4 * i : 4 * i + 4, :, 2 * FB : FFN] = sum_f[i].reshape(4, 8, FB)
    for k in range(1, 8):
        t, target = line_peer(me, k)
        one = copy(sums.at[t], grads.at[p], lfs.at[k], lfr.at[p], target)
        one.start()
        sent.append(one)

    @pl.when(core == 0)
    def _():
        asum.relay()

    sum_a = asum.finish()
    sum_b = jnp.zeros((64, 256), F32)
    entry = jnp.zeros((8, 128), F32)
    for k in range(1, 16):
        t, target = plane_peer(me, k)
        copy(got1.at[t], bland.at[t], bs.at[k], br.at[t], target).wait_recv()
        copy(ent.at[t], eland.at[t], es.at[k], er.at[t], target).wait_recv()
    for t in range(16):
        sum_b = sum_b + bland[t].astype(F32)
        entry = entry + eland[t]
    last = lax.broadcasted_iota(jnp.int32, (4, 8, 128), 1) == 7
    for i in range(2):
        added = jnp.where(last, entry[4 * i : 4 * i + 4].reshape(4, 1, 128), 0.0)
        narrow = sum_b[32 * i : 32 * i + 32].reshape(4, 8, 256)
        wide_rows = jnp.concatenate(
            [sum_a[i].reshape(4, 8, D), narrow[:, :, 0:128] + added, narrow[:, :, 128:256], jnp.zeros((4, 8, 128), F32)],
            axis=2,
        )
        asums[4 * i : 4 * i + 4] = jnp.concatenate(
            [wide_rows[:, :, 0:640], wide_rows[:, :, 640:1280]], axis=1
        ).astype(BF)
    for k in range(1, 8):
        t, target = line_peer(me, k)
        one = copy(asums.at[t], aland.at[p], las.at[k], lar.at[p], target)
        one.start()
        sent.append(one)
    aland[p] = asums[p]
    grads[p] = sums[p]
    result[...] = dot_nt((h[...] + ysum.finish()).astype(BF), spread[...]).astype(BF)
    io.leave(0)
    rest = dh[...] + dx_part
    total = jnp.zeros((TOK, D), F32)
    for _ in range(3):
        part = rest.astype(BF)
        total = total + dot_nt(part, spread[...])
        rest = rest - part.astype(F32)
    input_grad[...] = total
    io.leave(1)
    for k in range(1, 8):
        t, target = line_peer(me, k)
        copy(sums.at[t], grads.at[t], lfs.at[k], lfr.at[t], target).wait_recv()
    square = jnp.zeros((8, 128), F32)
    for t in range(8):
        square = square + fold_squares(grads[t])
    io.leave(2)
    for k in range(1, 8):
        t, target = line_peer(me, k)
        copy(asums.at[t], aland.at[t], las.at[k], lar.at[t], target).wait_recv()
    totals = []
    for side in range(2):
        both = aland[side].astype(F32)
        for t in range(1, 4):
            both = both + aland[side + 2 * t].astype(F32)
        totals.append(jnp.concatenate([both[0:8], both[8:16]], axis=1)[:, 0:ATT])
    eighth = lax.broadcasted_iota(jnp.int32, (8, ATT), 0) == 7
    totals = [totals[0] + jnp.where(eighth, totals[1], 0.0), jnp.where(eighth, 0.0, totals[1])]
    for side in range(2):
        att_grads[side] = totals[side]
        square = square + fold_squares(totals[side])
    io.leave(3)
    squares[0] = square
    lsq[p] = square
    for k in range(1, 8):
        t, target = line_peer(me, k)
        one = copy(squares.at[0], lsq.at[p], qs.at[k], qr.at[p], target)
        one.start()
        sent.append(one)
    for k in range(1, 8):
        t, target = line_peer(me, k)
        copy(squares.at[0], lsq.at[t], qs.at[k], qr.at[t], target).wait_recv()
    line_total = lsq[0]
    for t in range(1, 8):
        line_total = line_total + lsq[t]
    squares[1] = line_total
    psq[q] = line_total
    for k in range(1, 16):
        t, target = plane_peer(me, k)
        one = copy(squares.at[1], psq.at[q], ts.at[k], tr.at[q], target)
        one.start()
        sent.append(one)
    for k in range(1, 16):
        t, target = plane_peer(me, k)
        copy(squares.at[1], psq.at[t], ts.at[k], tr.at[t], target).wait_recv()
    full = psq[0]
    for t in range(1, 16):
        full = full + psq[t]
    norm[...] = full

    @pl.when(core == 1)
    def _():
        give_part(0, 1).wait_send()
        give_part(1, 1).wait_send()

    for one in sent:
        one.wait_send()
    for j in range(2):
        kv_pair(j).wait_send()
        kv_sums[j].drain()
    for ring in nears:
        ring.drain()
    fsum.drain()
    asum.drain()
    for k in range(1, 16):
        t, target = plane_peer(me, k)
        copy(got1.at[t], bland.at[q], bs.at[k], br.at[q], target).wait_send()
    ysum.drain()


def backward(*args):
    row = pltpu.VMEM
    return comm_call(
        backward_kernel,
        (
            shape(TOK, D), shape(TOK, D, dtype=F32), shape(8, 8, FFN, dtype=F32), shape(2, 8, ATT, dtype=F32),
            shape(8, 128, dtype=F32),
        ),
        [
            row((2, TOK // 2, DP), BF), row((2, TOK, DP), BF),
            row((2, 4, 4, 32, D), BF), row((16, 64, 256), BF), row((2, 4, 4, 32, D), BF), row((16, 64, 256), BF),
            row((16, 64, 256), BF), row((16, 8, 128), F32), row((16, 8, 128), F32),
            row((8, 16, 640), BF), row((8, 16, 640), BF), row((8, 8, FFN), F32), row((2, 8, 128), F32),
            row((8, 8, 128), F32), row((16, 8, 128), F32),
            row((2, 8 * TOK, 128), BF), row((TOK, D), BF),
            row((HEADS, TOK, 128), BF), row((8, HD, 2 * TOK), BF), row((8, HD, 2 * TOK), BF),
            row((HEADS, TOK, 128), F32), row((128, 8 * TOK), F32), row((128, 8 * TOK), F32),
            row((2, 2, TOK, 8 * TOK), BF), row((3 * TOK, 8 * TOK), BF),
            row((2, 4, 2, 128, TOK), BF), row((2, 2, 128, TOK), BF), row((2, 2, 2, 128, TOK), BF),
            row((2, 2, 128, TOK), BF), row((2, 128, TOK), BF),
            row((TOK, DP), F32), row((TOK, QKV), BF), row((TOK, DP), F32),
            row((2, 2, 16, 2 * FB), BF), row((2, 2, 32, 2 * FB), BF), dma(2, 6), dma(2, 6),
            *plane_sum_scratch(FB), *plane_sum_scratch(D),
            dma(2), dma(16), dma(16), dma(16), dma(16), dma(6), dma(6), dma(2, 2), dma(2, 2), dma(2, 6), dma(2, 6), dma(2), dma(2),
            dma(8), dma(8), dma(8), dma(8), dma(8), dma(8), dma(16), dma(16),
        ],
        3, *args, far_in=(22,), late=15,
    )


def adam_step(master, first_moment, second_moment, gradient, factor, step_rate, weight_decay):
    clipped = gradient * factor
    first_new = BETA_ONE * first_moment + (1.0 - BETA_ONE) * clipped
    second_new = BETA_TWO * second_moment + (1.0 - BETA_TWO) * clipped * clipped
    direction = (
        first_new
        / (1.0 - BETA_ONE**STEP)
        / (jnp.sqrt(second_new / (1.0 - BETA_TWO**STEP)) + ADAM_EPS)
    )
    master_new = master - step_rate * (direction + weight_decay * master)
    return (master_new, first_new, second_new, master_new.astype(jnp.bfloat16))


def update_kernel(io, squares, grads, att, spread, *refs):
    params, (result_in, input_in) = refs[0:24], refs[24:26]
    outs, (norm, result, input_grad) = refs[26:58], refs[58:61]
    io.arrive()
    result[...] = result_in[...]
    input_grad[...] = input_in[...]
    io.leave(33)
    io.leave(34)
    grad_norm = jnp.sqrt(jnp.sum(jnp.sum(squares[...], axis=0, keepdims=True), axis=1, keepdims=True))
    norm[...] = grad_norm
    factor = CLIP / jnp.maximum(grad_norm, CLIP)

    def step(number, gradient, first, columns):
        lanes = slice(first, first + columns)
        rate = STEP_RATES[number]
        decay = 0.0 if number == 7 else DECAY
        news = adam_step(*(params[3 * number + n][:, lanes] for n in range(3)), gradient, factor, rate, decay)
        for n in range(4):
            outs[4 * number + n][:, lanes] = news[n]

    def done(number):
        for n in range(4):
            io.leave(4 * number + n)

    for n in range(3):
        for t in range(8):
            first, width = (FB * t, FB) if t < 6 else (FB * 6 + 512 * (t - 6), 512)
            start = FB * n
            step(4 + n, grads[t, 0:7, start : start + width], first, width)
        done(4 + n)
    step(0, att[0, 0:7, 0:D], 0, D)
    step(1, att[0, 0:7, D : D + 128], 0, 128)
    step(2, att[0, 0:7, D + 128 : QKV], 0, 128)
    step(7, att[0, 7:8, D : D + NVEC], 0, NVEC)
    for number in (0, 1, 2, 7):
        done(number)
    rest = att[1, :, 0:DP]
    own = jnp.zeros((8, D), F32)
    for _ in range(3):
        part = rest.astype(BF)
        own = own + dot_nt(part, spread[...])
        rest = rest - part.astype(F32)
    step(3, own[0:7], 0, D)


def update(squares, grads, att, spread, params, result, input_grad):
    outs = []
    for number in range(8):
        dims = params[3 * number].shape
        outs += [shape(*dims, dtype=F32)] * 3 + [shape(*dims)]
    outs += [shape(1, 1, dtype=F32), shape(TOK, D), shape(TOK, D, dtype=F32)]
    return comm_call(update_kernel, tuple(outs), [], None, squares, grads, att, spread, *params, result, input_grad)


def per_device(
    tokens, cotangent, layout,
    w_query, m_query, v_query, w_key, m_key, v_key, w_value, m_value, v_value, w_out, m_out, v_out,
    w_gate, m_gate, v_gate, w_up, m_up, v_up, w_down, m_down, v_down, w_vectors, m_vectors, v_vectors,
):
    spread = jnp.asarray(spread_matrix(), BF)
    pick, spots, holds = (jnp.asarray(table, BF) for table in vector_tables())
    turns = jnp.asarray(turn_tables())
    h, n2, o_nat, invp, o_low, vec, cos, sin, n1, x, dy, q_ext, keys, values, wqkv, wo, wdn, wf, dyg, p_far = forward(
        layout, w_query, w_key, w_value, w_vectors[None], w_out, spread, w_gate, w_up, w_down,
        tokens[0], cotangent[0], turns, pick, spots, holds,
    )
    dn2, reduced, y_parts, ffn_grads = feed_forward(n2, wf, dyg, wdn)
    result, input_grad, grads, att, squares = backward(
        reduced, ffn_grads, y_parts, dn2, h, dy, vec, o_low, wo, spread, invp, o_nat, q_ext, keys, values, n1, x, wqkv,
        cos, sin, spots, holds, p_far,
    )
    params = [
        w_query, m_query, v_query, w_key, m_key, v_key, w_value, m_value, v_value, w_out, m_out, v_out,
        w_gate, m_gate, v_gate, w_up, m_up, v_up, w_down, m_down, v_down,
        w_vectors[None], m_vectors[None], v_vectors[None],
    ]
    *news, norm, result, input_grad = update(squares, grads, att, spread, params, result, input_grad)
    return (result[None], input_grad[None], norm[0, 0], *news[:28], *(one[0] for one in news[28:]))


def solution(mesh):
    token_spec = P("fsdp", "ctx", None)
    row_spec = P(("ctx", "fsdp"), None)
    vector_spec = P(("ctx", "fsdp"))
    in_specs = (token_spec, token_spec, P("fsdp", None)) + (row_spec,) * 21 + (vector_spec,) * 3
    out_specs = (token_spec, token_spec, P()) + (row_spec,) * 28 + (vector_spec,) * 4
    return jax.shard_map(
        per_device, mesh=mesh, in_specs=in_specs, out_specs=out_specs, check_vma=False
    )
```

```python
import jax
import jax.numpy as jnp
import numpy as np
from jax import lax
from jax.experimental import pallas as pl
from jax.experimental.pallas import tpu as pltpu
from jax.sharding import PartitionSpec as P

HEADS = 14
KV_HEADS = 2
HD = 64
PROMPT = 1024
CONT = 512
PIECE = 64
KBLK = 512
STEP = 10
D = 896
FF = 4864
TOK = 256
DP = 1024
FB = 640
QKV = 1152
ATT = 1152
FFN = 3 * FB
COLS = ATT + FFN
NVEC = 23
LANES = 2 * DP + QKV
LOG_E = 1.4426950408889634
A1 = 640
A2 = 512
HALF = COLS // 2

EPS_NORM = 1e-06
THETA = 1000000.0
CLIP = 1.0
BETA_ONE = 0.9
BETA_TWO = 0.95
ADAM_EPS = 1e-08
STEP_RATES = (0.02, 0.02, 0.02, 0.2, 0.02, 0.02, 0.02, 0.5)
DECAY = 0.1
MASKED = -1e30
MESH = pl.DeviceIdType.MESH
BF = jnp.bfloat16
F32 = jnp.float32
VMEM_LIMIT = 60 * 1024 * 1024


def owner_order():
    order = np.zeros((DP,), np.int32) - 1
    for x in range(4):
        for y in range(4):
            for z in range(4):
                for core in range(2):
                    p = z * 2 + core
                    owner = ((y % 2) * 4 + x) * 16 + z * 4 + (y // 2) * 2 + core
                    block = y * 4 + x if p < 4 else x * 4 + y
                    start = (p // 4) * 512 + block * 32 + (p % 4) * 8
                    order[start : start + 7] = np.arange(7 * owner, 7 * owner + 7)
    return order


def spread_matrix():
    order = owner_order()
    out = np.zeros((D, DP), np.float32)
    for column in range(DP):
        if order[column] >= 0:
            out[order[column], column] = 1.0
    return out

def vector_tables():
    order = owner_order()
    natural = np.concatenate([order, np.where(order < 0, -1, order + D), np.arange(2 * D, 2 * D + QKV)])
    owner_at = np.zeros((128,), np.int32)
    pick = np.zeros((128, DP), np.float32)
    for n in range(128):
        c, f = n // 16, n % 16
        owner_at[n] = ((f // 2 % 2 * 2 + c // 4) * 4 + c % 4) * 8 + f // 4 * 2 + f % 2
        pick[owner_at[n], np.nonzero(order == 7 * n)[0][0] + 7] = 1.0
    holds = np.zeros((128, LANES), np.float32)
    spots = np.zeros((128, LANES), np.float32)
    for lane in range(LANES):
        if natural[lane] >= 0:
            holds[owner_at[natural[lane] // NVEC], lane] = 1.0
            spots[natural[lane] % NVEC, lane] = 1.0
    return pick, spots, holds


def turn_tables():
    frequency = THETA ** (-(np.arange(HD // 2) * (2.0 / HD)))
    out = np.zeros((4, 64, 128), np.float32)
    for n, step in enumerate((PIECE, 1)):
        angles = np.arange(64)[:, None] * float(step) * frequency[None, :]
        out[2 * n] = np.tile(np.cos(angles), (1, 4))
        out[2 * n + 1] = np.tile(np.sin(angles), (1, 4))
    return out


def place():
    c = lax.axis_index("ctx")
    f = lax.axis_index("fsdp")
    return c % 4, (f // 2) % 2 * 2 + c // 4, f // 4, f % 2


def device(x, y, z, core):
    return {"ctx": y % 2 * 4 + x, "fsdp": z * 4 + y // 2 * 2 + core}


def x_peer(me, k):
    x, y, z, core = me
    return device((x + k) % 4, y, z, core)


def y_peer(me, k):
    x, y, z, core = me
    return device(x, (y + k) % 4, z, core)


def z_peer(me, k):
    x, y, z, core = me
    return device(x, y, (z + k) % 4, core)


def pair_peer(me):
    x, y, z, core = me
    return device(x, y // 2 * 2 + 1 - y % 2, z, core)


def other_core(me):
    x, y, z, core = me
    return device(x, y, z, 1 - core)


def line_peer(me, k):
    x, y, z, core = me
    t = (z * 2 + core + k) % 8
    return t, device(x, y, t // 2, t % 2)


def copy(src, dst, send, recv, target):
    return pltpu.make_async_remote_copy(
        src_ref=src, dst_ref=dst, send_sem=send, recv_sem=recv, device_id=target, device_id_type=MESH
    )


def greet(targets):
    barrier = pltpu.get_barrier_semaphore()
    for target in targets:
        pl.semaphore_signal(barrier, inc=1, device_id=target, device_id_type=MESH)
    pl.semaphore_wait(barrier, len(targets))


def line_targets(me):
    return [line_peer(me, k)[1] for k in range(1, 8)]


def ring_targets(me, peer):
    return [peer(me, 1), peer(me, 3)]


class Ring:
    def __init__(self, me, axis, block, half, send, recv):
        self.at = me[axis]
        self.up = (x_peer, y_peer, z_peer)[axis](me, 1)
        self.down = (x_peer, y_peer, z_peer)[axis](me, 3)
        self.half, self.send, self.recv = half, send, recv
        self.close = False

    def one(self, number, arriving=False):
        a = self.at
        ahead, behind, far = (a + 1) % 4, (a + 3) % 4, (a + 2) % 4
        half = (0, 1, 1, 0, 0, 1)[number]
        if arriving:
            t = (behind, behind, ahead, ahead, far, far)[number]
        else:
            t = (a, a, a, a, behind, ahead)[number]
        target = (self.up, self.up, self.down, self.down, self.up, self.down)[number]
        ref = self.half(t, half)
        return copy(ref, ref, self.send.at[number], self.recv.at[number], target)

    def start(self):
        for number in (0, 2, 1, 3):
            self.one(number).start()

    def relay(self):
        self.one(0, True).wait_recv()
        self.one(4).start()
        self.one(2, True).wait_recv()
        self.one(5).start()

    def near(self):
        self.close = True
        self.one(1, True).wait_recv()
        self.one(3, True).wait_recv()

    def finish(self):
        if not self.close:
            self.near()
        self.one(4, True).wait_recv()
        self.one(5, True).wait_recv()

    def drain(self):
        for number in range(6):
            self.one(number).wait_send()


def add_into(ref, other):
    ref[...] = ref[...] + other[...]


class RingSum:
    def __init__(self, me, axis, block, half, tmp, land, land_half, send, recv):
        self.at = me[axis]
        self.up = (x_peer, y_peer, z_peer)[axis](me, 1)
        self.down = (x_peer, y_peer, z_peer)[axis](me, 3)
        self.block, self.half, self.tmp = block, half, tmp
        self.land, self.land_half = land, land_half
        self.send, self.recv = send, recv

    def one(self, number):
        far, ahead, behind = (self.at + 2) % 4, (self.at + 1) % 4, (self.at + 3) % 4
        src, dst, target = (
            (self.half(far, 0), self.tmp(0), self.up), (self.half(far, 1), self.tmp(1), self.down),
            (self.half(ahead, 1), self.land_half(0, 1), self.up),
            (self.half(behind, 0), self.land_half(1, 0), self.down),
            (self.half(ahead, 0), self.land_half(0, 0), self.up),
            (self.half(behind, 1), self.land_half(1, 1), self.down),
        )[number]
        return copy(src, dst, self.send.at[number], self.recv.at[number], target)

    def start_far(self):
        self.one(0).start()
        self.one(1).start()

    def start_near(self):
        self.one(2).start()
        self.one(3).start()

    def start(self):
        self.start_far()
        self.start_near()

    def relay(self):
        ahead, behind = (self.at + 1) % 4, (self.at + 3) % 4
        self.one(0).wait_recv()
        add_into(self.half(ahead, 0), self.tmp(0))
        self.one(4).start()
        self.one(1).wait_recv()
        add_into(self.half(behind, 1), self.tmp(1))
        self.one(5).start()

    def finish(self):
        for number in range(2, 6):
            self.one(number).wait_recv()
        own = self.block(self.at)[...].astype(F32)
        return own + self.land(0)[...].astype(F32) + self.land(1)[...].astype(F32)

    def drain(self):
        for number in range(6):
            self.one(number).wait_send()


class PlaneGather:
    def __init__(self, me, first, second, send, recv):
        x, y, z, core = me

        def rows(ref, a, b, i):
            return ref.at[a, b, pl.ds(16 * i, 16)]

        self.near = [
            Ring(me, 0, lambda t: first.at[y, t], lambda t, i: rows(first, y, t, i), send.at[0], recv.at[0]),
            Ring(me, 1, lambda t: second.at[x, t], lambda t, i: rows(second, x, t, i), send.at[1], recv.at[1]),
        ]
        self.wide = [
            Ring(me, 1, lambda t: first.at[t], lambda t, i: first.at[t, pl.ds(2 * i, 2)], send.at[2], recv.at[2]),
            Ring(me, 0, lambda t: second.at[t], lambda t, i: second.at[t, pl.ds(2 * i, 2)], send.at[3], recv.at[3]),
        ]

    def start(self):
        for ring in self.near:
            ring.start()

    def relay(self):
        for ring in self.near:
            ring.relay()

    def widen(self):
        for one, two in zip(self.near, self.wide):
            one.finish()
            two.start()

    def relay_wide(self):
        for ring in self.wide:
            ring.relay()

    def finish(self):
        for ring in self.wide:
            ring.finish()

    def drain(self):
        for ring in self.near + self.wide:
            ring.drain()


class PlaneSum:
    def __init__(self, me, first, second, tmp_wide, land_wide, tmp, land, send, recv):
        x, y, z, core = me
        self.place = (y, x)
        self.refs = (first, second)

        def wide(axis, ref, n):
            return RingSum(
                me, axis, lambda t: ref.at[t], lambda t, i: ref.at[t, pl.ds(2 * i, 2)],
                lambda i: tmp_wide.at[n, i], lambda i: land_wide.at[n, i],
                lambda i, j: land_wide.at[n, i, pl.ds(2 * j, 2)], send.at[n], recv.at[n],
            )

        def near(axis, ref, a, n):
            return RingSum(
                me, axis, lambda t: ref.at[a, t], lambda t, i: ref.at[a, t, pl.ds(16 * i, 16)],
                lambda i: tmp.at[n, i], lambda i: land.at[n, i],
                lambda i, j: land.at[n, i, pl.ds(16 * j, 16)], send.at[2 + n], recv.at[2 + n],
            )

        self.wide = [wide(1, first, 0), wide(0, second, 1)]
        self.near = [near(0, first, y, 0), near(1, second, x, 1)]

    def start(self):
        for ring in self.wide:
            ring.start()

    def relay_wide(self):
        for ring in self.wide:
            ring.relay()

    def narrow(self):
        for number in range(2):
            total = self.wide[number].finish()
            self.refs[number][self.place[number]] = total.astype(BF)
            self.near[number].start()

    def relay(self):
        for ring in self.near:
            ring.relay()

    def finish(self):
        return [ring.finish() for ring in self.near]

    def drain(self):
        for ring in self.wide + self.near:
            ring.drain()


def plane_sum_scratch(columns):
    return [
        pltpu.VMEM((2, 2, 2, 32, columns), BF), pltpu.VMEM((2, 2, 4, 32, columns), BF),
        pltpu.VMEM((2, 2, 16, columns), BF), pltpu.VMEM((2, 2, 32, columns), BF),
        pltpu.SemaphoreType.DMA((4, 6)), pltpu.SemaphoreType.DMA((4, 6)),
    ]


class LineGather:
    def __init__(self, me, slots, send, recv, csend, crecv):
        self.me, self.slots, self.csend, self.crecv = me, slots, csend, crecv
        x, y, z, core = me
        half = slots.shape[1] // 2
        self.ring = Ring(
            me, 2, lambda t: slots.at[t * 2 + core],
            lambda t, i: slots.at[t * 2 + core, pl.ds(half * i, half)], send, recv,
        )

    def cross(self, k, mine=True):
        x, y, z, core = self.me
        t = (z + k) % 4
        ref = self.slots.at[t * 2 + (core if mine else 1 - core)]
        return copy(ref, ref, self.csend.at[t], self.crecv.at[t], other_core(self.me))

    def start(self):
        self.ring.start()
        self.cross(0).start()

    def relay(self):
        self.ring.relay()
        self.ring.near()
        self.cross(1).start()
        self.cross(3).start()

    def finish_far(self):
        self.ring.finish()
        self.cross(2).start()

    def wait(self, k):
        self.cross(k, False).wait_recv()

    def drain(self):
        self.ring.drain()
        for k in range(4):
            self.cross(k).wait_send()


def line_gather_sems():
    return [dma(6), dma(6), dma(4), dma(4)]


def dma(*n):
    return pltpu.SemaphoreType.DMA(n) if n else pltpu.SemaphoreType.DMA


class Io:
    def __init__(self, ins, outs, in_sem, out_sem):
        self.ins = [pltpu.make_async_copy(far, near, in_sem.at[n]) for n, (far, near) in enumerate(ins)]
        self.outs = [pltpu.make_async_copy(near, far, out_sem.at[n]) for n, (near, far) in enumerate(outs)]
        self.here = 0
        self.left = []

    def start(self, first, last=None):
        for one in self.ins[first:last]:
            one.start()

    def arrive(self, number=None):
        number = len(self.ins) if number is None else number
        while self.here < number:
            self.ins[self.here].wait()
            self.here += 1

    def leave(self, number):
        self.outs[number].start()
        self.left.append(number)

    def close(self):
        self.arrive()
        for number in range(len(self.outs)):
            if number not in self.left:
                self.leave(number)
        for number in self.left:
            self.outs[number].wait()


def comm_call(kernel, out_shape, scratch, number, *args, far_in=(), far_out=(), scalar_in=(), late=None):
    near_in = [n for n in range(len(args)) if n not in far_in and n not in scalar_in]
    near_out = [n for n in range(len(out_shape)) if n not in far_out]

    def body(*refs):
        ins, refs = list(refs[: len(args)]), refs[len(args) :]
        outs, refs = list(refs[: len(out_shape)]), refs[len(out_shape) :]
        near = refs[: len(near_in) + len(near_out)]
        rest, sems = refs[len(near) : -2], refs[-2:]
        io = Io(
            [(ins[n], near[i]) for i, n in enumerate(near_in)],
            [(near[len(near_in) + i], outs[n]) for i, n in enumerate(near_out)],
            *sems,
        )
        io.start(0, late)
        for i, n in enumerate(near_in):
            ins[n] = near[i]
        for i, n in enumerate(near_out):
            outs[n] = near[len(near_in) + i]
        kernel(io, *ins, *outs, *rest)
        io.close()

    spaces = [pltpu.VMEM(args[n].shape, args[n].dtype) for n in near_in]
    spaces += [pltpu.VMEM(out_shape[n].shape, out_shape[n].dtype) for n in near_out]
    if number is None:
        params = pltpu.CompilerParams(vmem_limit_bytes=VMEM_LIMIT)
    else:
        params = pltpu.CompilerParams(
            collective_id=number, has_side_effects=True, vmem_limit_bytes=VMEM_LIMIT
        )
    return pl.pallas_call(
        body,
        out_shape=out_shape,
        in_specs=[pl.BlockSpec(memory_space=pltpu.SMEM if n in scalar_in else pl.ANY) for n in range(len(args))],
        out_specs=tuple(pl.BlockSpec(memory_space=pl.ANY) for _ in out_shape),
        scratch_shapes=[*spaces, *scratch, dma(max(len(near_in), 1)), dma(max(len(near_out), 1))],
        compiler_params=params,
    )(*args)


def shape(*dims, dtype=BF):
    return jax.ShapeDtypeStruct(dims, dtype)


def scale_of(rows):
    return lax.rsqrt(jnp.sum(rows * rows, axis=-1, keepdims=True) * (1.0 / D) + EPS_NORM)


def norm_back(grad, rows, scale, gain):
    weighted = grad * gain
    mean = jnp.sum(weighted * rows, axis=-1, keepdims=True) * (1.0 / D)
    return scale * weighted - rows * (scale * scale * scale * mean), jnp.sum(grad * rows * scale, axis=0)


def dot(left, right):
    return jnp.dot(left, right, preferred_element_type=F32)


def dot_tn(left, right):
    return lax.dot_general(left, right, (((0,), (0,)), ((), ())), preferred_element_type=F32)


def dot_nt(left, right):
    return lax.dot_general(left, right, (((1,), (1,)), ((), ())), preferred_element_type=F32)


def lane(rows):
    return lax.broadcasted_iota(jnp.int32, (rows, 128), 1)


def swap_halves(value):
    low = lane(value.shape[0]) % HD < HD // 2
    return jnp.where(low, pltpu.roll(value, 128 - HD // 2, 1), pltpu.roll(value, HD // 2, 1))


def rope(value, cos, sin):
    return value * cos + swap_halves(value) * sin


def side_of(value, side):
    return jnp.where(lane(value.shape[0]) // HD == side, value, 0.0)


def moved(value, source, target):
    shifted = value if source == target else pltpu.roll(value, HD, 1)
    return side_of(shifted, target)


def local_copy(src, dst, sem):
    return pltpu.make_async_copy(src, dst, sem)


def piece_code(piece):
    later = piece - PROMPT // PIECE
    tail = 4096 * (later // (CONT // PIECE) + 1) + PROMPT + later % (CONT // PIECE) * PIECE
    return jnp.where(later < 0, piece * PIECE, tail)


def forward_kernel(
    io, layout, wq, wk, wv, wvec, wo, spread, wg, wu, wd, tok, cot, turns, pick, spots, holds,
    h_out, n2_out, o_nat, invp, o_low, vec, cos, sin, n1_s, x_s, dy_s, q_ext, keys, values, wa, wb, wdn, wf, dyg, p_far,
    msg, land, msg_b, land_b, w8, pk, s_a, s_b, k_s, v_s, o_ext, p_a, p_b, marks,
    s1s, s1r, s2s, s2r, dns, dnr, fs, fr, as_, ar, bs, br, ls, lr, lcs, lcr, cs, cr, kps, kpr, kxs, kxr, vps, vpr, vxs, vxr, own_sem, p_sem,
):
    me = place()
    x, y, z, core = me
    p = z * 2 + core
    low = y % 2
    greet(line_targets(me) + ring_targets(me, x_peer) + ring_targets(me, y_peer))
    io.arrive(4)

    firsts = []

    def hand_round(out, arrived, send, recv):
        for k in range(1, 8):
            t, target = line_peer(me, k)
            one = copy(out.at[t], arrived.at[p], send.at[k], recv.at[p], target)
            one.start()
            firsts.append(one)
        arrived[p] = out[p]

    def collect(out, arrived, send, recv):
        for k in range(1, 8):
            t, target = line_peer(me, k)
            copy(out.at[t], arrived.at[t], send.at[k], recv.at[t], target).wait_recv()

    def folded(whole, columns):
        return jnp.concatenate([whole[:, :columns], whole[:, columns:]], axis=0).astype(BF)

    def unfolded(arrived, j):
        a = arrived[2 * j].astype(F32)
        b = arrived[2 * j + 1].astype(F32)
        return jnp.concatenate([jnp.concatenate([a[:8], b[:8]], 0), jnp.concatenate([a[8:], b[8:]], 0)], 1).astype(BF)

    def blank(columns):
        return jnp.zeros((8, columns), F32)

    w8[...] = jnp.zeros_like(w8)
    first = 0
    for ref in (wq, wk, wv):
        w8[0:7, first : first + ref.shape[1]] = ref[...]
        first += ref.shape[1]
    w8[7:8, 0:NVEC] = wvec[...]
    halves = (
        folded(jnp.concatenate([w8[:, 0:A1], blank(128)], 1), 384),
        folded(jnp.concatenate([w8[:, A1:QKV], blank(256)], 1), 384),
    )
    for t in range(8):
        msg[t] = halves[t % 2]
    hand_round(msg, land, s1s, s1r)
    io.arrive(9)
    w8[0:7, QKV : QKV + DP] = dot(wo[...].astype(BF), spread[...])
    for n, ref in enumerate((wg, wu, wd)):
        w8[0:7, QKV + DP + FF * n : QKV + DP + FF * (n + 1)] = ref[...]
    for t in range(8):
        base = QKV + DP + FB * t if t < 6 else QKV + DP + FB * 6 + 512 * (t - 6)
        width = FB if t < 6 else 512
        at = QKV + A2 * (t % 2)
        pieces = [w8[:, at : at + A2]]
        for n in range(3):
            pieces.append(w8[:, base + FF * n : base + FF * n + width])
            if width < FB:
                pieces.append(blank(FB - width))
        pieces.append(blank(128))
        msg_b[t] = folded(jnp.concatenate(pieces, axis=1), 1280)
    hand_round(msg_b, land_b, s2s, s2r)
    io.arrive()
    x_s[...] = dot(tok[...], spread[...])
    io.leave(9)
    dy_s[...] = dot(cot[...], spread[...]).astype(BF)
    io.leave(10)
    own_dy = local_copy(dy_s, dyg.at[p], own_sem.at[2])
    own_dy.start()
    collect(msg, land, s1s, s1r)
    for j in range(4):
        rows = slice(16 * (j % 2), 16 * (j % 2) + 16)
        at = (y, x) if j < 2 else (x, y)
        wa[core, j // 2, at[0], at[1], rows, :] = unfolded(land, j)[:, 0:A1]
    att = PlaneGather(me, wa.at[core, 0], wa.at[core, 1], as_, ar)
    out = PlaneGather(me, wb.at[core, 0], wb.at[core, 1], bs, br)
    ffn = PlaneGather(me, wf.at[0], wf.at[1], fs, fr)
    down = [
        Ring(me, n, lambda t, n=n: None, lambda t, i, n=n: wdn.at[n, t, pl.ds(16 * i, 16)], dns.at[n], dnr.at[n])
        for n in range(2)
    ]
    line = LineGather(me, dyg, ls, lr, lcs, lcr)
    att.start()
    codes = jnp.zeros((1, 128), jnp.int32)
    for t in range(32):
        block = t // 4
        code = piece_code(layout[0, (block % 2 * 4 + block // 2) * 4 + t % 4])
        codes = jnp.where(lane(1) % HD == t, code, codes)
    sign = jnp.where(lane(PIECE) % HD < HD // 2, -1.0, 1.0)
    for i in range(4):
        code = piece_code(layout[0, 4 * (low * 4 + x) + i])
        rows = slice(PIECE * i, PIECE * i + PIECE)
        seen = (codes <= code) & ((codes < PROMPT) | (codes >= code // 4096 * 4096))
        barred = jnp.where((lane(1) % HD < 32) & jnp.logical_not(seen), MASKED, 0.0)
        marks[rows, :] = jnp.zeros((PIECE, 128), F32) + barred
        number = code % 4096 // PIECE
        cos_far, sin_far = turns[0, pl.ds(number, 1), :], turns[1, pl.ds(number, 1), :]
        cos_near, sin_near = turns[2, 0:PIECE, :], turns[3, 0:PIECE, :]
        cos[rows, :] = cos_far * cos_near - sin_far * sin_near
        sin[rows, :] = (sin_far * cos_near + cos_far * sin_near) * sign
    io.leave(6)
    io.leave(7)
    att.relay()
    own_dy.wait()
    line.start()
    att.widen()
    collect(msg_b, land_b, s2s, s2r)
    for j in range(4):
        rows = slice(16 * (j % 2), 16 * (j % 2) + 16)
        at = (y, x) if j < 2 else (x, y)
        block = unfolded(land_b, j)
        wb[core, j // 2, at[0], at[1], rows, :] = block[:, 0:A2]
        pk[j // 2, rows, :] = block[:, A2 : A2 + 2 * FB]
        wdn[j // 2, (x, y)[j // 2], rows, :] = block[:, A2 + 2 * FB : A2 + FFN]
    out.start()
    owns = [
        local_copy(pk.at[0], wf.at[0, y, x], own_sem.at[0]), local_copy(pk.at[1], wf.at[1, x, y], own_sem.at[1])
    ]
    for one in owns:
        one.start()
    att.relay_wide()
    out.relay()
    for one in owns:
        one.wait()
    ffn.start()
    att.finish()
    cross = [
        copy(ref.at[core], ref.at[core], cs.at[n], cr.at[n], other_core(me)) for n, ref in enumerate((wa, wb))
    ]
    crossed = [
        copy(ref.at[1 - core], ref.at[1 - core], cs.at[n], cr.at[n], other_core(me)) for n, ref in enumerate((wa, wb))
    ]
    cross[0].start()
    out.widen()
    crossed[0].wait_recv()

    table = dot(pick[...], wide(wa, 0, 0, 128)).astype(BF)
    vec[...] = jnp.sum(dot(table, spots[...]) * holds[...].astype(F32), axis=0, keepdims=True)
    xs = x_s[...]
    n1_s[...] = (xs * scale_of(xs) * vec[:, 0:DP]).astype(BF)
    second = dot(n1_s[...], wide(wa, 1, 0, QKV - A1)) + vec[:, 2 * DP + A1 :]
    kv_pre = second[:, D - A1 :]
    keys[x, low] = rope(kv_pre[:, 0:128], cos[...], sin[...]).astype(BF)
    values[x, low] = kv_pre[:, 128:256].astype(BF)
    key_pair = copy(keys.at[x, low], keys.at[x, low], kps, kpr, pair_peer(me))
    key_pair.start()
    key_ring = Ring(me, 0, lambda t: keys.at[t], lambda t, i: keys.at[t, i], kxs, kxr)
    value_ring = Ring(
        me, 0, lambda t: values.at[t, low], lambda t, i: values.at[t, low, pl.ds(128 * i, 128)], vxs, vxr
    )
    value_ring.start()
    value_pair = copy(values.at[:, low], values.at[:, low], vps, vpr, pair_peer(me))
    io.leave(5)
    io.leave(8)
    io.leave(14)
    q_pre = jnp.concatenate(
        [dot(n1_s[...], wide(wa, 0, 0, A1)) + vec[:, 2 * DP : 2 * DP + A1], second[:, : D - A1]], axis=1
    )
    copy(keys.at[x, 1 - low], keys.at[x, 1 - low], kps, kpr, pair_peer(me)).wait_recv()
    key_ring.start()
    value_ring.relay()
    for head in range(HEADS):
        block = q_pre[:, 128 * (head // 2) : 128 * (head // 2) + 128]
        turned = rope(block, cos[...], sin[...]) * (HD**-0.5 * LOG_E)
        turned = moved(turned, head % 2, head // 7)
        q_ext[head] = (turned + side_of(marks[...], 1 - head // 7)).astype(BF)
    io.leave(11)
    value_ring.finish()
    value_pair.start()
    key_ring.relay()
    out.relay_wide()
    ffn.relay()
    ffn.widen()
    line.relay()
    key_ring.finish()
    io.leave(12)
    out.finish()
    cross[1].start()
    for ring in down:
        ring.start()
    all_keys = keys[...].reshape(8 * TOK, 128).astype(F32)
    piece = lax.broadcasted_iota(jnp.int32, (8 * TOK, 128), 0) // PIECE
    marked = jnp.where(lane(8 * TOK) % HD == piece, 1.0, 0.0)
    for j in range(2):
        k_s[j] = jnp.where(lane(8 * TOK) // HD == j, all_keys, marked).astype(BF)
    apart = lax.broadcasted_iota(jnp.int32, (TOK, TOK), 1) - lax.broadcasted_iota(jnp.int32, (TOK, TOK), 0)
    same = lax.broadcasted_iota(jnp.int32, (TOK, TOK), 1) // PIECE == lax.broadcasted_iota(jnp.int32, (TOK, TOK), 0) // PIECE
    diagonal = pl.ds(pl.multiple_of((x * 2 + low) * TOK, TOK), TOK)
    copy(values.at[:, 1 - low], values.at[:, 1 - low], vps, vpr, pair_peer(me)).wait_recv()
    io.leave(13)
    v_s[:, 0:128] = values[...].reshape(8 * TOK, 128)
    v_s[:, 128:256] = jnp.ones((8 * TOK, 128), BF)
    invp[...] = jnp.zeros_like(invp)

    p_s = (p_a, p_b)
    s_s = (s_a, s_b)

    def put(i, j):
        return local_copy(p_s[j].at[i % 2], p_far.at[7 * j + i], p_sem.at[j, i % 2])

    def attend(i, carry):
        @pl.when(i >= 2)
        def _():
            for j in range(2):
                put(i, j).wait()

        for j in range(2):
            s_s[j][...] = dot_nt(q_ext[7 * j + i], k_s[j])
        inverse_all = invp[...]
        for j in range(2):
            s_s[j][:, diagonal] = jnp.where(same & (apart > 0), MASKED, s_s[j][:, diagonal])
            scores = s_s[j][...]
            numerators = jnp.exp2(scores - jnp.max(scores, axis=1, keepdims=True)).astype(BF)
            p_s[j][i % 2] = numerators
            both = dot(numerators, v_s[...])
            inverse = 1.0 / both[:, 128:256]
            o_ext[7 * j + i] = side_of(both[:, 0:128] * inverse, j)
            inverse_all = jnp.where(lane(TOK) == 7 * j + i, inverse, inverse_all)
        invp[...] = inverse_all
        for j in range(2):
            put(i, j).start()
        return carry

    lax.fori_loop(0, 4, attend, 0)
    crossed[1].wait_recv()
    io.leave(15)
    ffn.relay_wide()
    for ring in down:
        ring.relay()
    line.finish_far()
    lax.fori_loop(4, 7, attend, 0)
    for block in range(7):
        pieces = [moved(o_ext[2 * block + e], (2 * block + e) // 7, e) for e in range(2)]
        o_nat[:, 128 * block : 128 * block + 128] = pieces[0] + pieces[1]

    o_low[...] = dot(o_nat[...].astype(BF), spread[...]).astype(BF)
    for n in range(2):
        cols = slice(A2 * n, A2 * n + A2)
        h_out[:, cols] = x_s[:, cols] + dot(o_low[...], wide(wb, n, 0, A2))
    h = h_out[...]
    n2_out[...] = (h * scale_of(h) * vec[:, DP : 2 * DP]).astype(BF)
    for number in range(5):
        io.leave(number)
    for ring in down:
        ring.finish()
    io.leave(16)
    ffn.finish()
    for k in range(4):
        line.wait(k)
    for i in (5, 6):
        for j in range(2):
            put(i, j).wait()
    line.drain()
    att.drain()
    out.drain()
    ffn.drain()
    for ring in down:
        ring.drain()
    key_ring.drain()
    value_ring.drain()
    key_pair.wait_send()
    value_pair.wait_send()
    for one in firsts + cross:
        one.wait_send()


def wide(ref, side, first, columns):
    return ref[side, :, :, :, :, first : first + columns].reshape(DP, columns)


def forward(*args):
    row = pltpu.VMEM
    return comm_call(
        forward_kernel,
        (
            shape(TOK, DP, dtype=F32), shape(TOK, DP), shape(TOK, D, dtype=F32), shape(TOK, 128, dtype=F32),
            shape(TOK, DP), shape(1, LANES, dtype=F32), shape(TOK, 128, dtype=F32), shape(TOK, 128, dtype=F32),
            shape(TOK, DP), shape(TOK, DP, dtype=F32), shape(TOK, DP), shape(HEADS, TOK, 128),
            shape(4, 2, TOK, 128), shape(4, 2, TOK, 128),
            shape(2, 2, 4, 4, 32, A1), shape(2, 2, 4, 4, 32, A2), shape(2, 4, 32, FB), shape(2, 4, 4, 32, 2 * FB),
            shape(8, TOK, DP), shape(HEADS, TOK, 8 * TOK),
        ),
        [
            row((8, 16, 384), BF), row((8, 16, 384), BF), row((8, 16, 1280), BF), row((8, 16, 1280), BF),
            row((8, QKV + DP + 3 * FF), F32), row((2, 32, 2 * FB), BF), row((TOK, 8 * TOK), F32),
            row((TOK, 8 * TOK), F32), row((2, 8 * TOK, 128), BF), row((8 * TOK, 256), BF),
            row((HEADS, TOK, 128), F32), row((2, TOK, 8 * TOK), BF), row((2, TOK, 8 * TOK), BF),
            row((TOK, 128), F32),
            dma(8), dma(8), dma(8), dma(8), dma(2, 6), dma(2, 6), dma(4, 6), dma(4, 6), dma(4, 6), dma(4, 6), dma(4, 6), dma(4, 6),
            *line_gather_sems(), dma(2), dma(2), dma(), dma(), dma(6), dma(6), dma(), dma(), dma(6), dma(6),
            dma(3), dma(2, 2),
        ],
        1, *args, far_out=(17, 18, 19), scalar_in=(0,),
    )


def ffn_kernel(
    io, n2, wf, dyg, wdn, dn2_out, reduced, y_far,
    wd, grads, grads_d, n2g, dparts, yparts, got, tmp, land, hid_all, dgu_all, dhid_all, gu_s,
    f_tw, f_lw, f_t, f_l, f_s, f_r, d_tw, d_lw, d_t, d_l, d_s, d_r, leave, wds, wdr, ls, lr, lcs, lcr, gs, gr, ds, dr,
):
    me = place()
    x, y, z, core = me
    rows = [
        pltpu.make_async_copy(wdn.at[0], wd.at[0, y], leave.at[0]),
        pltpu.make_async_copy(wdn.at[1], wd.at[1, x], leave.at[1]),
    ]
    for one in rows:
        one.start()
    greet(ring_targets(me, z_peer) + [other_core(me)] + ring_targets(me, x_peer) + ring_targets(me, y_peer))
    io.arrive(1)
    n2g[z * 2 + core] = n2[...]
    line = LineGather(me, n2g, ls, lr, lcs, lcr)
    line.start()
    for one in rows:
        one.wait()
    gathers = [
        Ring(
            me, 1 - n, lambda t: None, lambda t, i, n=n: wd.at[n, t, pl.ds(2 * i, 2)], wds.at[n], wdr.at[n]
        )
        for n in range(2)
    ]
    for ring in gathers:
        ring.start()

    def both():
        return wf[...].reshape(DP, 2 * FB)

    def down():
        return wd[...].reshape(DP, FB)

    def slot(k, side):
        return (z + k) % 4 * 2 + side

    def one(s, gu=None):
        gu = dot(n2g[s], both()) if gu is None else gu
        gate, up = gu[:, :FB], gu[:, FB:]
        sig = 1.0 / (1.0 + jnp.exp(-gate))
        act = gate * sig
        hid_all[s] = (act * up).astype(BF)
        dhid = dhid_all[s]
        dgu_all[s, :, :FB] = (dhid * up * (sig + act * (1.0 - sig))).astype(BF)
        dgu_all[s, :, FB:] = (dhid * act).astype(BF)
        dparts[s] = dot_nt(dgu_all[s], both()).astype(BF)

    def pair(n, ref, k):
        t = (z + k) % 4
        return copy(ref.at[t * 2 + 1 - core], got.at[n, t], gs.at[n, t], gr.at[n, t], other_core(me))

    def join(n, ref, k):
        t = (z + k) % 4
        pair(n, ref, k).wait_recv()
        add_into(ref.at[t * 2 + core], got.at[n, t])

    def compute(k, between=None):
        if between is None:

            def body(i, carry):
                side = (1 - core) * (1 - i) + core * i
                one(slot(k, side), gu_s[side] if k == 0 else None)
                return carry

            lax.fori_loop(0, 2, body, 0)
        else:
            lax.fori_loop(0, 1, lambda i, carry: (one(slot(k, 1 - core)), carry)[1], 0)
            between()
            lax.fori_loop(0, 1, lambda i, carry: (one(slot(k, core)), carry)[1], 0)
        pair(0, dparts, k).start()

    dsum = RingSum(
        me, 2, lambda t: dparts.at[t * 2 + core], lambda t, i: dparts.at[t * 2 + core, pl.ds(128 * i, 128)],
        lambda i: tmp.at[i], lambda i: land.at[i], lambda i, j: land.at[i, pl.ds(128 * j, 128)], ds, dr,
    )

    def after_first():
        join(0, dparts, 1)
        dsum.one(2).start()

    def after_far():
        join(0, dparts, 2)
        dsum.start_far()

    def hidden_grads(first, last):
        def body(i, carry):
            s = (z * 2 + i) % 8
            dhid_all[s] = dot(dyg[s], down())
            return carry

        lax.fori_loop(first, last, body, 0)

    def own_gates(side, carry):
        gu_s[side] = dot(n2g[z * 2 + side], both())
        return carry

    io.arrive()
    line.wait(0)
    lax.fori_loop(0, 2, own_gates, 0)
    for ring in gathers:
        ring.relay()
    for ring in gathers:
        ring.finish()
    hidden_grads(0, 2)
    compute(0)
    hidden_grads(2, 8)
    line.relay()
    line.wait(1)
    line.wait(3)
    compute(1)
    join(0, dparts, 0)
    line.finish_far()
    line.wait(2)
    compute(2, after_first)
    compute(3, after_far)

    fsum = PlaneSum(me, grads.at[0], grads.at[1], f_tw, f_lw, f_t, f_l, f_s, f_r)
    down_sum = PlaneSum(me, grads_d.at[0], grads_d.at[1], d_tw, d_lw, d_t, d_l, d_s, d_r)
    leaves = []

    def weight_grads(left, right, into, width, first, last):
        for m in range(first, last):
            rows = left[:, :, 256 * m : 256 * m + 256].reshape(8 * TOK, 256)
            value = dot_tn(rows, right[...].reshape(8 * TOK, width)).astype(BF)
            into[m // 2, 2 * (m % 2) : 2 * (m % 2) + 2] = value.reshape(2, 4, 32, width)

    def outputs(k, carry):
        for side in range(2):
            yparts[slot(k, side)] = dot_nt(hid_all[slot(k, side)], down()).astype(BF)
        return carry

    weight_grads(n2g, dgu_all, grads, 2 * FB, 0, 1)
    join(0, dparts, 3)
    dsum.one(3).start()
    weight_grads(n2g, dgu_all, grads, 2 * FB, 1, 2)
    fsum.wide[0].start()
    weight_grads(n2g, dgu_all, grads, 2 * FB, 2, 4)
    fsum.wide[1].start()
    dsum.relay()
    weight_grads(dyg, hid_all, grads_d, FB, 0, 4)
    down_sum.start()
    fsum.wide[0].relay()
    lax.fori_loop(0, 2, outputs, 0)
    for k in range(2):
        pair(1, yparts, k).start()
    fsum.wide[1].relay()
    dn2_out[...] = dsum.finish()
    io.leave(0)
    lax.fori_loop(2, 4, outputs, 0)
    for k in range(2, 4):
        pair(1, yparts, k).start()
    down_sum.relay_wide()
    for k in range(4):
        join(1, yparts, k)
        t = (z + k) % 4
        one_out = pltpu.make_async_copy(yparts.at[t * 2 + core], y_far.at[t], leave.at[k])
        one_out.start()
        leaves.append(one_out)
    for n in range(2):
        reduced[n, :, :, 0 : 2 * FB] = fsum.wide[n].finish().astype(BF)
        reduced[n, :, :, 2 * FB : FFN] = down_sum.wide[n].finish().astype(BF)
    io.leave(1)
    for ring in fsum.wide + down_sum.wide + gathers:
        ring.drain()
    line.drain()
    for n, ref in enumerate((dparts, yparts)):
        for k in range(4):
            pair(n, ref, k).wait_send()
    dsum.drain()
    for one_out in leaves:
        one_out.wait()


def feed_forward(n2, wf, dyg, wdn):
    slots = pltpu.VMEM((8, TOK, DP), BF)
    return comm_call(
        ffn_kernel,
        (shape(TOK, DP, dtype=F32), shape(2, 4, 32, FFN), shape(4, TOK, DP)),
        [
            pltpu.VMEM((2, 4, 4, 32, FB), BF), pltpu.VMEM((2, 4, 4, 32, 2 * FB), BF), pltpu.VMEM((2, 4, 4, 32, FB), BF),
            slots, slots, slots, pltpu.VMEM((2, 4, TOK, DP), BF),
            pltpu.VMEM((2, TOK // 2, DP), BF), pltpu.VMEM((2, TOK, DP), BF),
            pltpu.VMEM((8, TOK, FB), BF), pltpu.VMEM((8, TOK, 2 * FB), BF), pltpu.VMEM((8, TOK, FB), F32),
            pltpu.VMEM((2, TOK, 2 * FB), F32),
            *plane_sum_scratch(2 * FB), *plane_sum_scratch(FB), dma(6), dma(2, 6), dma(2, 6),
            *line_gather_sems(), dma(2, 4), dma(2, 4), dma(6), dma(6),
        ],
        2, n2, wf, dyg, wdn, far_in=(3,), far_out=(2,),
    )


def plane_peer(me, k):
    x, y, z, core = me
    t = (y * 4 + x + k) % 16
    return t, device(t % 4, t // 4, z, core)


def fold_squares(value):
    total = jnp.zeros((8, 128), F32)
    for b in range(value.shape[1] // 128):
        piece = value[:, 128 * b : 128 * b + 128]
        total = total + piece * piece
    return total


def backward_kernel(
    io, reduced, yb, dn2, h, dy, vec, o_low, wb, spread, invp, o_nat, q_ext, k_s, v_in,
    n1, xs, wa, cos, sin, spots, holds, p_far,
    result, input_grad, grads, att_grads, norm,
    ytmp, yland, ag0, ag1, got0, got1, bland, ent, eland, asums, aland, sums, squares, lsq, psq,
    v_s, do_s, do_ext, do_t, q_t, dq_ext, dkt, dvt, p_s, ds_s, kvp, kvtmp, kvland, give, take, dh, dqkv, dn1,
    n_t, n_l, n_s, n_r, a_tw, a_lw, a_t, a_l, a_s, a_r,
    p_sem, bs, br, es, er, ys, yr, cs, cr, ks, kr, kps, kpr, lfs, lfr, las, lar, qs, qr, ts, tr,
):
    me = place()
    x, y, z, core = me
    p = z * 2 + core
    q = y * 4 + x
    low = y % 2

    units = [(0, 2), (2, 2), (4, 2), (6, 1), (7, 2), (9, 2), (11, 2), (13, 1)]

    def get(unit):
        head, count = units[unit]
        rows = pl.ds(0, count)
        return local_copy(p_far.at[pl.ds(head, count)], p_s.at[unit % 2, rows], p_sem.at[unit % 2])

    for unit in range(2):
        get(unit).start()
    io.start(14)
    greet(line_targets(me) + [plane_peer(me, k)[1] for k in range(1, 16)])
    io.arrive(2)
    asum = PlaneSum(me, got0.at[0], got0.at[1], a_tw, a_lw, a_t, a_l, a_s, a_r)

    def send_narrow():
        for k in range(1, 16):
            t, target = plane_peer(me, k)
            copy(got1.at[t], bland.at[q], bs.at[k], br.at[q], target).start()
        bland[q] = got1[q]

    def by_place(value):
        for t in range(16):
            turned = t % 4 * 4 + t // 4
            yield t, value[32 * t : 32 * t + 32], value[512 + 32 * turned : 544 + 32 * turned]

    ysum = RingSum(
        me, 2, lambda t: yb.at[t], lambda t, i: yb.at[t, pl.ds(128 * i, 128)],
        lambda i: ytmp.at[i], lambda i: yland.at[i], lambda i, j: yland.at[i, pl.ds(128 * j, 128)], ys, yr,
    )
    nears = [
        RingSum(
            me, n, lambda t, n=n: reduced.at[n, t], lambda t, i, n=n: reduced.at[n, t, pl.ds(16 * i, 16)],
            lambda i, n=n: n_t.at[n, i], lambda i, n=n: n_l.at[n, i],
            lambda i, j, n=n: n_l.at[n, i, pl.ds(16 * j, 16)], n_s.at[n], n_r.at[n],
        )
        for n in range(2)
    ]
    for ring in nears:
        ring.start()
    ysum.start()

    io.arrive(9)
    scale_two = scale_of(h[...])
    dh_part, dgain_two = norm_back(dn2[...], h[...], scale_two, vec[:, DP : 2 * DP])
    dh[...] = dy[...].astype(F32) + dh_part
    da = dh[...].astype(BF)
    dwo = dot_tn(o_low[...], da).astype(BF)
    ag0[...] = dwo[:, 0:D].reshape(2, 4, 4, 32, D)
    ag1[...] = jnp.zeros_like(ag1)
    for t, one, two in by_place(dwo[:, D:DP]):
        ag1[t, 0:32, 0:128] = one
        ag1[t, 32:64, 0:128] = two

    def give_part(n, number):
        return copy((ag0, ag1)[n], (got0, got1)[n], cs.at[number, n], cr.at[number, n], other_core(me))

    @pl.when(core == 0)
    def _():
        give_part(0, 0).start()
        give_part(1, 0).start()

    do_far = (dot_nt(da[:, 0:A2], wide(wb, 0, 0, A2)) + dot_nt(da[:, A2:DP], wide(wb, 1, 0, A2))).astype(BF)
    do_s[...] = dot_nt(do_far, spread[...]).astype(BF)
    io.arrive(14)
    all_values = v_in[...].reshape(8 * TOK, 128).astype(F32)
    for j in range(2):
        ones = jnp.where(lane(8 * TOK) % HD < 3, 1.0, 0.0)
        v_s[j] = jnp.where(lane(8 * TOK) // HD == j, all_values, ones).astype(BF)

    def prepare(unit):
        first, count = units[unit]
        for spot in range(count):
            head = first + spot
            j = head // 7
            lanes = slice(128 * (head // 2), 128 * (head // 2) + 128)
            inverse = invp[:, head : head + 1]
            block = side_of(do_s[:, lanes].astype(F32), head % 2)
            rest = -jnp.sum(block * o_nat[:, lanes], axis=1, keepdims=True) * inverse
            value = moved(block * inverse, head % 2, j)
            for n in range(3):
                part = rest.astype(BF).astype(F32)
                value = jnp.where(lane(TOK) == HD * (1 - j) + n, part, value)
                rest = rest - part
            do_ext[head] = value.astype(BF)
            columns = slice(TOK * spot, TOK * spot + TOK)
            do_t[unit, :, columns] = value.T[HD * j : HD * j + HD].astype(BF)
            q_t[unit, :, columns] = q_ext[head].astype(F32).T[HD * j : HD * j + HD].astype(BF)

    for ring in nears:
        ring.relay()
    prepare(0)
    dkt[...] = jnp.zeros_like(dkt)
    dvt[...] = jnp.zeros_like(dvt)

    @pl.when(core == 1)
    def _():
        give_part(0, 0).wait_recv()
        add_into(got0, ag0)
        asum.start()
        give_part(1, 0).wait_recv()
        add_into(got1, ag1)
        send_narrow()

    def heads(unit):
        head, count = units[unit]
        j = head // 7
        half = slice(HD * j, HD * j + HD)
        rows = count * TOK
        base = 2 * TOK if unit == 7 else 0
        get(unit).wait()
        dp = dot_nt(do_ext[head : head + count].reshape(rows, 128), v_s[j])
        numerators = p_s[unit % 2, 0:count].reshape(rows, 8 * TOK)
        dvt[half, :] += dot(do_t[unit, :, 0:rows], numerators)
        ds_s[base : base + rows, :] = dp.astype(BF) * numerators
        if unit + 1 < len(units):
            prepare(unit + 1)
        dkt[half, :] += dot(q_t[unit, :, 0:rows], ds_s[base : base + rows, :])
        if unit < 6:
            query_grads(head, count)
        if unit + 2 < len(units):
            get(unit + 2).start()

    def query_grads(head, count):
        value = dot(ds_s[0 : count * TOK, :], k_s[...].reshape(8 * TOK, 128))
        dq_ext[head : head + count] = value.reshape(count, TOK, 128)

    def kv_sum(j):
        return RingSum(
            me, 0, lambda t: kvp.at[j, t], lambda t, i: kvp.at[j, t, i],
            lambda i: kvtmp.at[j, i], lambda i: kvland.at[j, i], lambda i, n: kvland.at[j, i, n],
            ks.at[j], kr.at[j],
        )

    def kv_pack(j):
        for t in range(8):
            lanes = slice(256 * t, 256 * t + 256)
            kvp[j, t // 2, t % 2, 0:HD, :] = (dkt[HD * j : HD * j + HD, lanes] * (1.0 / LOG_E)).astype(BF)
            kvp[j, t // 2, t % 2, HD:128, :] = dvt[HD * j : HD * j + HD, lanes].astype(BF)

    def kv_pair(j):
        return copy(give.at[j, 1 - low], take.at[j], kps.at[j], kpr.at[j], pair_peer(me))

    def kv_cross(j):
        give[j] = kv_sums[j].finish().astype(BF)
        kv_pair(j).start()

    def kv_total(j):
        kv_pair(j).wait_recv()
        return give[j, low].astype(F32) + take[j].astype(F32)

    kv_sums = [kv_sum(0), kv_sum(1)]
    heads(0)
    heads(1)
    ysum.relay()

    @pl.when(core == 1)
    def _():
        asum.relay_wide()

    heads(2)
    heads(3)
    kv_pack(0)
    kv_sums[0].start()

    @pl.when(core == 1)
    def _():
        asum.narrow()

    heads(4)
    heads(5)
    kv_sums[0].relay()

    @pl.when(core == 1)
    def _():
        asum.relay()

    heads(6)
    kv_cross(0)
    heads(7)
    kv_pack(1)
    kv_sums[1].start()

    query_grads(11, 3)
    io.arrive()
    for block in range(7):
        pieces = [moved(dq_ext[2 * block + e], (2 * block + e) // 7, e) for e in range(2)]
        turned = rope((pieces[0] + pieces[1]) * HD**-0.5, cos[...], -sin[...])
        dqkv[:, 128 * block : 128 * block + 128] = turned.astype(BF)
    @pl.when(core == 0)
    def _():
        give_part(0, 0).wait_send()
        give_part(1, 0).wait_send()

    ag0[...] = dot_tn(n1[...], dqkv[:, 0:D]).astype(BF).reshape(2, 4, 4, 32, D)

    @pl.when(core == 1)
    def _():
        give_part(0, 1).start()

    kv_sums[1].relay()
    dn1[...] = dot_nt(dqkv[:, 0:A1], wide(wa, 0, 0, A1)) + dot_nt(dqkv[:, A1:D], wide(wa, 1, 0, D - A1))
    kv_cross(1)

    @pl.when(core == 0)
    def _():
        give_part(0, 1).wait_recv()
        add_into(got0, ag0)
        asum.start()

    dkv = [kv_total(0), kv_total(1)]
    dk = jnp.concatenate([dkv[0][0:HD], dkv[1][0:HD]], axis=0).T
    dv = jnp.concatenate([dkv[0][HD:128], dkv[1][HD:128]], axis=0).T
    dqkv[:, D : D + 128] = rope(dk, cos[...], -sin[...]).astype(BF)
    dqkv[:, D + 128 : QKV] = dv.astype(BF)
    for t, one, two in by_place(dot_tn(n1[...], dqkv[:, D:QKV]).astype(BF)):
        ag1[t, 0:32] = one
        ag1[t, 32:64] = two

    @pl.when(core == 1)
    def _():
        give_part(1, 1).start()

    @pl.when(core == 0)
    def _():
        asum.relay_wide()
        give_part(1, 1).wait_recv()
        add_into(got1, ag1)
        send_narrow()

    dn1_all = dn1[...] + dot_nt(dqkv[:, D:QKV], wide(wa, 1, D - A1, QKV - D))
    scale_one = scale_of(xs[...])
    dx_part, dgain_one = norm_back(dn1_all, xs[...], scale_one, vec[:, 0:DP])
    dbias = jnp.sum(dqkv[...].astype(F32), axis=0, keepdims=True)
    dvec = jnp.concatenate([dgain_one[None], dgain_two[None], dbias], axis=1)
    dvec_high = dvec.astype(BF).astype(F32)
    entries = jnp.zeros((128, 128), F32)
    for part in (dvec_high, dvec - dvec_high):
        entries = entries + dot_nt((holds[...].astype(F32) * part).astype(BF), spots[...])
    ent[...] = entries.reshape(16, 8, 128)
    sent = []
    for k in range(1, 16):
        t, target = plane_peer(me, k)
        one = copy(ent.at[t], eland.at[q], es.at[k], er.at[q], target)
        one.start()
        sent.append(one)
    eland[q] = ent[q]

    @pl.when(core == 0)
    def _():
        asum.narrow()

    for i in range(2):
        sums[4 * i : 4 * i + 4] = nears[i].finish().reshape(4, 8, FFN)
    for k in range(1, 8):
        t, target = line_peer(me, k)
        one = copy(sums.at[t], grads.at[p], lfs.at[k], lfr.at[p], target)
        one.start()
        sent.append(one)

    @pl.when(core == 0)
    def _():
        asum.relay()

    sum_a = asum.finish()
    sum_b = jnp.zeros((64, 256), F32)
    entry = jnp.zeros((8, 128), F32)
    for k in range(1, 16):
        t, target = plane_peer(me, k)
        copy(got1.at[t], bland.at[t], bs.at[k], br.at[t], target).wait_recv()
        copy(ent.at[t], eland.at[t], es.at[k], er.at[t], target).wait_recv()
    for t in range(16):
        sum_b = sum_b + bland[t].astype(F32)
        entry = entry + eland[t]
    last = lax.broadcasted_iota(jnp.int32, (4, 8, 128), 1) == 7
    for i in range(2):
        added = jnp.where(last, entry[4 * i : 4 * i + 4].reshape(4, 1, 128), 0.0)
        narrow = sum_b[32 * i : 32 * i + 32].reshape(4, 8, 256)
        wide_rows = jnp.concatenate(
            [sum_a[i].reshape(4, 8, D), narrow[:, :, 0:128] + added, narrow[:, :, 128:256], jnp.zeros((4, 8, 128), F32)],
            axis=2,
        )
        asums[4 * i : 4 * i + 4] = jnp.concatenate(
            [wide_rows[:, :, 0:640], wide_rows[:, :, 640:1280]], axis=1
        ).astype(BF)
    for k in range(1, 8):
        t, target = line_peer(me, k)
        one = copy(asums.at[t], aland.at[p], las.at[k], lar.at[p], target)
        one.start()
        sent.append(one)
    aland[p] = asums[p]
    grads[p] = sums[p]
    result[...] = dot_nt((h[...] + ysum.finish()).astype(BF), spread[...]).astype(BF)
    io.leave(0)
    rest = dh[...] + dx_part
    total = jnp.zeros((TOK, D), F32)
    for _ in range(3):
        part = rest.astype(BF)
        total = total + dot_nt(part, spread[...])
        rest = rest - part.astype(F32)
    input_grad[...] = total
    io.leave(1)
    for k in range(1, 8):
        t, target = line_peer(me, k)
        copy(sums.at[t], grads.at[t], lfs.at[k], lfr.at[t], target).wait_recv()
    square = jnp.zeros((8, 128), F32)
    for t in range(8):
        square = square + fold_squares(grads[t])
    io.leave(2)
    for k in range(1, 8):
        t, target = line_peer(me, k)
        copy(asums.at[t], aland.at[t], las.at[k], lar.at[t], target).wait_recv()
    totals = []
    for side in range(2):
        both = aland[side].astype(F32)
        for t in range(1, 4):
            both = both + aland[side + 2 * t].astype(F32)
        totals.append(jnp.concatenate([both[0:8], both[8:16]], axis=1)[:, 0:ATT])
    eighth = lax.broadcasted_iota(jnp.int32, (8, ATT), 0) == 7
    totals = [totals[0] + jnp.where(eighth, totals[1], 0.0), jnp.where(eighth, 0.0, totals[1])]
    for side in range(2):
        att_grads[side] = totals[side]
        square = square + fold_squares(totals[side])
    io.leave(3)
    squares[0] = square
    lsq[p] = square
    for k in range(1, 8):
        t, target = line_peer(me, k)
        one = copy(squares.at[0], lsq.at[p], qs.at[k], qr.at[p], target)
        one.start()
        sent.append(one)
    for k in range(1, 8):
        t, target = line_peer(me, k)
        copy(squares.at[0], lsq.at[t], qs.at[k], qr.at[t], target).wait_recv()
    line_total = lsq[0]
    for t in range(1, 8):
        line_total = line_total + lsq[t]
    squares[1] = line_total
    psq[q] = line_total
    for k in range(1, 16):
        t, target = plane_peer(me, k)
        one = copy(squares.at[1], psq.at[q], ts.at[k], tr.at[q], target)
        one.start()
        sent.append(one)
    for k in range(1, 16):
        t, target = plane_peer(me, k)
        copy(squares.at[1], psq.at[t], ts.at[k], tr.at[t], target).wait_recv()
    full = psq[0]
    for t in range(1, 16):
        full = full + psq[t]
    norm[...] = full

    @pl.when(core == 1)
    def _():
        give_part(0, 1).wait_send()
        give_part(1, 1).wait_send()

    for one in sent:
        one.wait_send()
    for j in range(2):
        kv_pair(j).wait_send()
        kv_sums[j].drain()
    for ring in nears:
        ring.drain()
    asum.drain()
    for k in range(1, 16):
        t, target = plane_peer(me, k)
        copy(got1.at[t], bland.at[q], bs.at[k], br.at[q], target).wait_send()
    ysum.drain()


def backward(*args):
    row = pltpu.VMEM
    return comm_call(
        backward_kernel,
        (
            shape(TOK, D), shape(TOK, D, dtype=F32), shape(8, 8, FFN, dtype=F32), shape(2, 8, ATT, dtype=F32),
            shape(8, 128, dtype=F32),
        ),
        [
            row((2, TOK // 2, DP), BF), row((2, TOK, DP), BF),
            row((2, 4, 4, 32, D), BF), row((16, 64, 256), BF), row((2, 4, 4, 32, D), BF), row((16, 64, 256), BF),
            row((16, 64, 256), BF), row((16, 8, 128), F32), row((16, 8, 128), F32),
            row((8, 16, 640), BF), row((8, 16, 640), BF), row((8, 8, FFN), F32), row((2, 8, 128), F32),
            row((8, 8, 128), F32), row((16, 8, 128), F32),
            row((2, 8 * TOK, 128), BF), row((TOK, D), BF),
            row((HEADS, TOK, 128), BF), row((8, HD, 2 * TOK), BF), row((8, HD, 2 * TOK), BF),
            row((HEADS, TOK, 128), F32), row((128, 8 * TOK), F32), row((128, 8 * TOK), F32),
            row((2, 2, TOK, 8 * TOK), BF), row((3 * TOK, 8 * TOK), BF),
            row((2, 4, 2, 128, TOK), BF), row((2, 2, 128, TOK), BF), row((2, 2, 2, 128, TOK), BF),
            row((2, 2, 128, TOK), BF), row((2, 128, TOK), BF),
            row((TOK, DP), F32), row((TOK, QKV), BF), row((TOK, DP), F32),
            row((2, 2, 16, FFN), BF), row((2, 2, 32, FFN), BF), dma(2, 6), dma(2, 6),
            *plane_sum_scratch(D),
            dma(2), dma(16), dma(16), dma(16), dma(16), dma(6), dma(6), dma(2, 2), dma(2, 2), dma(2, 6), dma(2, 6), dma(2), dma(2),
            dma(8), dma(8), dma(8), dma(8), dma(8), dma(8), dma(16), dma(16),
        ],
        3, *args, far_in=(21,), late=14,
    )


def adam_step(master, first_moment, second_moment, gradient, factor, step_rate, weight_decay):
    clipped = gradient * factor
    first_new = BETA_ONE * first_moment + (1.0 - BETA_ONE) * clipped
    second_new = BETA_TWO * second_moment + (1.0 - BETA_TWO) * clipped * clipped
    direction = (
        first_new
        / (1.0 - BETA_ONE**STEP)
        / (jnp.sqrt(second_new / (1.0 - BETA_TWO**STEP)) + ADAM_EPS)
    )
    master_new = master - step_rate * (direction + weight_decay * master)
    return (master_new, first_new, second_new, master_new.astype(jnp.bfloat16))


def update_kernel(io, result_in, input_in, squares, grads, att, spread, *refs):
    params = refs[0:24]
    outs, (norm, result, input_grad) = refs[24:56], refs[56:59]
    io.arrive(2)
    result[...] = result_in[...]
    io.leave(33)
    input_grad[...] = input_in[...]
    io.leave(34)
    io.arrive(6)
    grad_norm = jnp.sqrt(jnp.sum(jnp.sum(squares[...], axis=0, keepdims=True), axis=1, keepdims=True))
    norm[...] = grad_norm
    io.leave(32)
    factor = CLIP / jnp.maximum(grad_norm, CLIP)

    def step(number, gradient, first, columns):
        lanes = slice(first, first + columns)
        rate = STEP_RATES[number]
        decay = 0.0 if number == 7 else DECAY
        news = adam_step(*(params[3 * number + n][:, lanes] for n in range(3)), gradient, factor, rate, decay)
        for n in range(4):
            outs[4 * number + n][:, lanes] = news[n]

    rest = att[1, :, 0:DP]
    own = jnp.zeros((8, D), F32)
    for _ in range(3):
        part = rest.astype(BF)
        own = own + dot_nt(part, spread[...])
        rest = rest - part.astype(F32)
    blocks = [
        [(att[0, 0:7, 0:D], 0, D)], [(att[0, 0:7, D : D + 128], 0, 128)], [(att[0, 0:7, D + 128 : QKV], 0, 128)],
        [(own[0:7], 0, D)],
    ]
    spans = [(FB * t, FB) if t < 6 else (FB * 6 + 512 * (t - 6), 512) for t in range(8)]
    for n in range(3):
        blocks.append(
            [(grads[t, 0:7, FB * n : FB * n + width], first, width) for t, (first, width) in enumerate(spans)]
        )
    blocks.append([(att[0, 7:8, D : D + NVEC], 0, NVEC)])
    for number in range(8):
        io.arrive(9 + 3 * number)
        for block in blocks[number]:
            step(number, *block)
        for n in range(4):
            io.leave(4 * number + n)


def update(squares, grads, att, spread, params, result, input_grad):
    outs = []
    for number in range(8):
        dims = params[3 * number].shape
        outs += [shape(*dims, dtype=F32)] * 3 + [shape(*dims)]
    outs += [shape(1, 1, dtype=F32), shape(TOK, D), shape(TOK, D, dtype=F32)]
    return comm_call(update_kernel, tuple(outs), [], None, result, input_grad, squares, grads, att, spread, *params)


def per_device(
    tokens, cotangent, layout,
    w_query, m_query, v_query, w_key, m_key, v_key, w_value, m_value, v_value, w_out, m_out, v_out,
    w_gate, m_gate, v_gate, w_up, m_up, v_up, w_down, m_down, v_down, w_vectors, m_vectors, v_vectors,
):
    spread = jnp.asarray(spread_matrix(), BF)
    pick, spots, holds = (jnp.asarray(table, BF) for table in vector_tables())
    turns = jnp.asarray(turn_tables())
    h, n2, o_nat, invp, o_low, vec, cos, sin, n1, x, dy, q_ext, keys, values, wqkv, wo, wdn, wf, dyg, p_far = forward(
        layout, w_query, w_key, w_value, w_vectors[None], w_out, spread, w_gate, w_up, w_down,
        tokens[0], cotangent[0], turns, pick, spots, holds,
    )
    dn2, reduced, y_parts = feed_forward(n2, wf, dyg, wdn)
    result, input_grad, grads, att, squares = backward(
        reduced, y_parts, dn2, h, dy, vec, o_low, wo, spread, invp, o_nat, q_ext, keys, values, n1, x, wqkv,
        cos, sin, spots, holds, p_far,
    )
    params = [
        w_query, m_query, v_query, w_key, m_key, v_key, w_value, m_value, v_value, w_out, m_out, v_out,
        w_gate, m_gate, v_gate, w_up, m_up, v_up, w_down, m_down, v_down,
        w_vectors[None], m_vectors[None], v_vectors[None],
    ]
    *news, norm, result, input_grad = update(squares, grads, att, spread, params, result, input_grad)
    return (result[None], input_grad[None], norm[0, 0], *news[:28], *(one[0] for one in news[28:]))


def solution(mesh):
    token_spec = P("fsdp", "ctx", None)
    row_spec = P(("ctx", "fsdp"), None)
    vector_spec = P(("ctx", "fsdp"))
    in_specs = (token_spec, token_spec, P("fsdp", None)) + (row_spec,) * 21 + (vector_spec,) * 3
    out_specs = (token_spec, token_spec, P()) + (row_spec,) * 28 + (vector_spec,) * 4
    return jax.shard_map(
        per_device, mesh=mesh, in_specs=in_specs, out_specs=out_specs, check_vma=False
    )
```
